512 devices in a mesh: dp: 16 (over z), seq: 32 (over y, x, core).
Axes of the slice: x: 4, y: 4, z: 16, core: 2. Of those that a mesh axis runs over, the one named last changes fastest.
Arguments:
- queries: bfloat16 [16, 4096, 2048], P('dp', 'seq'), may hold values from -6 to 6
- keys: bfloat16 [16, 4096, 2048], P('dp', 'seq'), may hold values from -6 to 6
- values: bfloat16 [16, 4096, 2048], P('dp', 'seq'), may hold values from -6 to 6
- residual_in: bfloat16 [16, 4096, 2048], P('dp', 'seq'), may hold values from -6 to 6
- cotangent: bfloat16 [16, 4096, 2048], P('dp', 'seq'), may hold values from -0.09375 to 0.09375
- expert_ids: int32 [16, 4096, 2], P('dp', 'seq'), may hold values from 0 to 31, all different within a row; in each aligned block of 128 rows (0 to 127, 128 to 255, ..., all dimensions but the last counted through in order) at most 12 rows name the same one
- router: bfloat16 [2048, 32], replicated, may hold values from -0.125 to 0.125
- attn_gain: float32 [2048], replicated, may hold values from 0.25 to 1.75
- moe_gain: float32 [2048], replicated, may hold values from 0.25 to 1.75
- w_gate: bfloat16 [32, 2048, 256], P('seq', 'dp'), may hold values from -0.125 to 0.125
- w_up: bfloat16 [32, 2048, 256], P('seq', 'dp'), may hold values from -0.125 to 0.125
- w_down: bfloat16 [32, 2048, 256], P('seq', 'dp'), may hold values from -0.375 to 0.375
- trainable: int32 [32], P('seq'), may hold values 0 or 1
Outputs:
- mixed: bfloat16 [16, 4096, 2048], P('dp', 'seq')
- grad_gate: float32 [32, 2048, 256], P('seq', 'dp')
- grad_up: float32 [32, 2048, 256], P('seq', 'dp')
- grad_down: float32 [32, 2048, 256], P('seq', 'dp')
The draws below stay inside these ranges and needn't reach their ends.
Inputs may be any that keep to these rules, and one draw needn't show every extreme that they name: `expert_ids`: each position names two different experts; among the 128 positions of one index of seq no expert is named by more than 12 choices, a bound that some block reaches.
All inputs are finite; a program needn't handle non-finite values. No bound on the sum of `trainable` on one device may be relied on, other than what follows from the above.
Results may differ from the reference program's by a relative error of at most 0.025.
Values may be sent and summed in bfloat16 or wider, within the bound.
A program may use at most 128 MiB of HBM per device.

```python
import math
import jax
import jax.numpy as jnp
import numpy as np
from jax import lax

D = 2048
HD = 128
FF = 256
TOK_DEV = 128
HEADS = 16
EXPERTS = 32
CAP = 12
GROUPS = 16
LENGTH = 4096
N_SEQ = 32


def with_ends(array, key, least, largest):
    index_at = [jax.random.randint(jax.random.fold_in(key, axis), (), 0, length) for axis, length in enumerate(array.shape)]
    longest = array.shape.index(max(array.shape))
    beside = index_at[:longest] + [(index_at[longest] + 1) % array.shape[longest]] + index_at[longest + 1:]
    return array.at[tuple(index_at)].set(least).at[tuple(beside)].set(largest)


def shard_levels(key, dims, shards, low, largest):
    def one(position, parts):
        draws = jax.random.uniform(jax.random.fold_in(jax.random.fold_in(key, 6), position), (parts,), jnp.float32, low / len(shards), largest / len(shards))
        return jnp.repeat(jnp.exp(draws), dims[position] // parts).reshape((-1,) + (1,) * (len(dims) - position - 1))

    factor_of = one(*shards[0])
    for cut in shards[1:]:
        factor_of = factor_of * one(*cut)
    return factor_of


def deal_out(rng, own, number, rows, count, top, bound, skew):
    sequence = jax.random.permutation(rng, count)
    heavy_load, common = portions_of(count, rows * top, bound, skew, True), portions_of(count, rows * top, bound, skew, False)
    places = jnp.arange(count)

    def named(lengths, rotation):
        used = int((lengths > 0).sum())
        fixed = max(1, used // 4)
        moved = fixed + (places - fixed + rotation * (used - fixed)) % max(1, count - fixed)
        return jnp.zeros((count,), jnp.int32).at[sequence[jnp.where(places < fixed, places, moved)]].set(jnp.asarray(lengths, jnp.int32))

    lengths = jnp.where(number % 4 == 0, named(heavy_load, number // 4), named(common, number - number // 4 - 1))
    mixed = jax.random.permutation(jax.random.fold_in(own, 3), count)
    donor, receiver = mixed[0:count // 2 * 2:2], mixed[1:count // 2 * 2:2]
    room = jnp.minimum(lengths[donor] - 1, bound - lengths[receiver]) // 2
    room = jnp.where((donor == sequence[0]) | (receiver == sequence[0]) | (lengths[receiver] == 0), 0, jnp.maximum(room, 0))
    moved = jax.random.randint(jax.random.fold_in(own, 4), (count // 2,), 0, 1 << 20) % (room + 1)
    lengths = lengths.at[donor].add(-moved).at[receiver].add(moved)
    items = jnp.searchsorted(jnp.cumsum(lengths), jnp.arange(rows * top), side="right").astype(jnp.int32)
    table = items.reshape(top, rows).T
    table = table[jax.random.permutation(jax.random.fold_in(own, 1), rows)]
    rotation = jax.random.randint(jax.random.fold_in(own, 2), (rows, 1), 0, top)
    return jnp.take_along_axis(table, (jnp.arange(top)[None, :] + rotation) % top, axis=1)


def portions_of(count, total, bound, lean, full):
    loads = [(1 << 20) // math.isqrt(grade ** lean) + 1 for grade in range(1, count + 1)]
    largest = bound if full else min(bound, max(-(-total // count), total * loads[0] // sum(loads)))
    least = 1 if total - largest >= count - 1 else 0
    holding, rest = [largest] + [least] * (count - 1), total - largest - least * (count - 1)
    while rest > 0:
        movable = [i for i in range(1, count) if holding[i] < largest] or [i for i in range(1, count) if holding[i] < bound]
        pool, remaining = sum([loads[i] for i in movable]), rest
        for i in movable:
            more = min(bound - holding[i], max(1, remaining * loads[i] // pool), rest)
            holding[i] = holding[i] + more
            rest = rest - more
    return np.array(holding)


def centred(own_key, dims, spread, reach, pieces=(), kind=jnp.bfloat16):
    result = spread * jax.random.normal(own_key, dims, jnp.float32)
    if pieces:
        result = result * shard_levels(own_key, dims, pieces, -0.22, 0.18)
    return jnp.clip(result, -reach, reach).astype(kind)


def setup_inputs(seed: int = 0) -> dict:
    splits = jax.random.split(jax.random.key(seed), 14)
    queries = centred(splits[0], (GROUPS, LENGTH, D), 1.0, 6.0, ((0, 16), (1, 32)))
    keys = centred(splits[1], (GROUPS, LENGTH, D), 1.0, 6.0, ((0, 16), (1, 32)))
    values = centred(splits[2], (GROUPS, LENGTH, D), 1.0, 6.0, ((0, 16), (1, 32)))
    residual_in = centred(splits[3], (GROUPS, LENGTH, D), 1.0, 6.0, ((0, 16), (1, 32)))
    cotangent = centred(splits[4], (GROUPS, LENGTH, D), 0.015625, 0.09375, ((0, 16), (1, 32)))
    expert_ids_keys = jax.random.split(jax.random.fold_in(splits[5], 1), GROUPS * LENGTH // TOK_DEV)
    expert_ids_turns = jax.random.permutation(jax.random.fold_in(splits[5], 3), GROUPS * LENGTH // TOK_DEV)
    expert_ids = jax.vmap(lambda own, number: deal_out(jax.random.fold_in(splits[5], 2), own, number, TOK_DEV, EXPERTS, 2, CAP, 2))(expert_ids_keys, expert_ids_turns).reshape((GROUPS, LENGTH, 2))
    router = centred(splits[6], (D, EXPERTS), D ** -0.5, 0.125)
    attn_gain = jnp.clip(1.0 + 0.15 * jax.random.normal(splits[7], (D,), jnp.float32), 0.25, 1.75)
    moe_gain = jnp.clip(1.0 + 0.15 * jax.random.normal(splits[8], (D,), jnp.float32), 0.25, 1.75)
    w_gate = centred(splits[9], (EXPERTS, D, FF), D ** -0.5, 0.125, ((0, 32), (1, 16)))
    w_up = centred(splits[10], (EXPERTS, D, FF), D ** -0.5, 0.125, ((0, 32), (1, 16)))
    w_down = centred(splits[11], (EXPERTS, D, FF), FF ** -0.5, 0.375, ((0, 32), (1, 16)))
    trainable = with_ends((jax.random.randint(splits[12], (EXPERTS,), 0, 2) < 1).astype(jnp.int32), jax.random.fold_in(splits[12], 1), 0, 1)
    return {"queries": queries, "keys": keys, "values": values, "residual_in": residual_in, "cotangent": cotangent, "expert_ids": expert_ids, "router": router, "attn_gain": attn_gain, "moe_gain": moe_gain, "w_gate": w_gate, "w_up": w_up, "w_down": w_down, "trainable": trainable}


def to_half(value):
    return lax.optimization_barrier(value.astype(jnp.bfloat16)).astype(jnp.float32)

def attend(queries, keys, values):
    shape = (N_SEQ, TOK_DEV, HEADS, HD)
    qf = queries.astype(jnp.float32).reshape(shape)
    kf = keys.astype(jnp.float32).reshape(shape)
    vf = values.astype(jnp.float32).reshape(shape)
    scores = jnp.einsum('cthd,cshd->chts', qf, kf)
    causal = jnp.tril(jnp.ones((TOK_DEV, TOK_DEV), dtype=bool))
    weights = to_half(jnp.where(causal, scores, 0.0))
    intra = jnp.einsum('chts,cshd->cthd', weights, vf)
    local = jnp.einsum('cthd,cthe->chde', kf, vf)
    prefix = jnp.concatenate([jnp.zeros_like(local[:1]), jnp.cumsum(local[:-1], axis=0)], axis=0)
    carried = jnp.einsum('cthd,chde->cthe', qf, prefix, precision=lax.Precision.HIGHEST)
    attended = intra + carried
    attended = attended * lax.rsqrt(lax.optimization_barrier(jnp.mean(attended * attended, axis=-1, keepdims=True)) + 1e-06)
    return attended.reshape(N_SEQ * TOK_DEV, D)

def one_group(carry, inputs, router, attn_gain, moe_gain, gate32, up32, down32):
    queries, keys, values, residual_in, cotangent, expert_ids = inputs
    length = queries.shape[0]
    stream = residual_in.astype(jnp.float32) + attend(queries, keys, values) * attn_gain
    normed = (stream * lax.rsqrt(lax.optimization_barrier(jnp.mean(stream * stream, axis=-1, keepdims=True)) + 1e-06) * moe_gain).astype(jnp.bfloat16)
    logits = jnp.dot(normed, router, preferred_element_type=jnp.float32)
    onehot = (expert_ids[..., None] == jnp.arange(EXPERTS, dtype=jnp.int32)).astype(jnp.int32)
    chosen = lax.optimization_barrier(jnp.sum(onehot.astype(jnp.float32) * logits[:, None, :], axis=-1))
    sig = jax.nn.sigmoid(chosen)
    gates = sig / lax.optimization_barrier(jnp.sum(sig, axis=-1, keepdims=True))
    flat = onehot.reshape(N_SEQ, 2 * TOK_DEV, EXPERTS)
    before = jnp.cumsum(flat, axis=1) - flat
    rank = lax.optimization_barrier(jnp.sum(before * flat, axis=-1)).astype(jnp.int32)
    chosen_ids = expert_ids.reshape(N_SEQ, 2 * TOK_DEV).astype(jnp.int32)
    rows = N_SEQ * CAP
    dest = (chosen_ids * rows + jnp.arange(N_SEQ, dtype=jnp.int32)[:, None] * CAP + rank).reshape(-1)
    repeated = jnp.repeat(normed, 2, axis=0)
    bucket = jnp.zeros((EXPERTS * rows, D), jnp.bfloat16).at[dest].set(repeated)
    expert_cot = (cotangent.astype(jnp.float32)[:, None, :] * gates[:, :, None]).reshape(2 * length, D).astype(jnp.bfloat16)
    cot_bucket = jnp.zeros((EXPERTS * rows, D), jnp.bfloat16).at[dest].set(expert_cot)
    xf = lax.optimization_barrier(bucket).astype(jnp.float32).reshape(EXPERTS, rows, D)
    dyf = lax.optimization_barrier(cot_bucket).astype(jnp.float32).reshape(EXPERTS, rows, D)
    pre_gate = jnp.einsum('erd,edf->erf', xf, gate32)
    pre_up = jnp.einsum('erd,edf->erf', xf, up32)
    sigma = jax.nn.sigmoid(pre_gate)
    act = pre_gate * sigma
    hidden = to_half(act * pre_up)
    expert_out = jnp.einsum('erf,edf->erd', hidden, down32).astype(jnp.bfloat16)
    gathered = expert_out.reshape(EXPERTS * rows, D)[dest].astype(jnp.float32).reshape(length, 2, D)
    mixed = (stream + lax.optimization_barrier(jnp.sum(gates[:, :, None] * gathered, axis=1))).astype(jnp.bfloat16)
    d_hidden = jnp.einsum('erd,edf->erf', dyf, down32)
    d_gate = to_half(d_hidden * pre_up * sigma * (1.0 + pre_gate * (1.0 - sigma)))
    d_up = to_half(d_hidden * act)
    part_gate = to_half(jnp.einsum('erd,erf->edf', xf, d_gate))
    part_up = to_half(jnp.einsum('erd,erf->edf', xf, d_up))
    part_down = to_half(jnp.einsum('erd,erf->edf', dyf, hidden))
    carry = (carry[0] + part_gate, carry[1] + part_up, carry[2] + part_down)
    return (carry, mixed)

def reference(queries, keys, values, residual_in, cotangent, expert_ids, router, attn_gain, moe_gain, w_gate, w_up, w_down, trainable):
    gate32 = w_gate.astype(jnp.float32)
    up32 = w_up.astype(jnp.float32)
    down32 = w_down.astype(jnp.float32)
    zeros = jnp.zeros((EXPERTS, D, FF), jnp.float32)

    def step(carry, inputs):
        return one_group(carry, inputs, router, attn_gain, moe_gain, gate32, up32, down32)
    totals, mixed = lax.scan(step, (zeros, zeros, zeros), (queries, keys, values, residual_in, cotangent, expert_ids))
    flag = (trainable > 0).astype(jnp.float32)[:, None, None]
    return (mixed, totals[0] * flag, totals[1] * flag, totals[2] * flag)
```

```python
import functools

import jax
import jax.numpy as jnp
from jax import lax
from jax.experimental import pallas as pl
from jax.experimental.pallas import tpu as pltpu
from jax.sharding import PartitionSpec as P

HD = 128
EPS = 1e-06
MESH = pl.DeviceIdType.MESH
F32 = jnp.float32
BF16 = jnp.bfloat16
Q = 4
GR = 4
SUB = 2


def dot(a, b, ca=1, cb=0):
    return lax.dot_general(a, b, (((ca,), (cb,)), ((), ())), preferred_element_type=F32)


def kernel(
    grid3,
    slots,
    q_ref,
    k_ref,
    v_ref,
    res_ref,
    cot_ref,
    ids_ref,
    router_ref,
    again_ref,
    mgain_ref,
    wg_ref,
    wu_ref,
    wd_ref,
    train_ref,
    mixed_ref,
    gg_ref,
    gu_ref,
    gd_ref,
    w_all,
    st_send,
    st_recv,
    pf_send,
    pf_recv,
    wq,
    stream,
    nst,
    place,
    placeg,
    c_send,
    c_recv,
    x_send,
    x_recv,
    g_send,
    g_recv,
    xs,
    cs,
    pre,
    gcol,
    dgu,
    hid,
    hidg,
    r_send,
    r_recv,
    rs_send,
    rs_recv,
    ag_ss,
    ag_rs,
    p_sem,
    c_ss,
    c_rs,
    x_ss,
    x_rs,
    g_sem,
    r_ss,
    r_rs,
    rr_ss,
    rr_rs,
):
    ny, nx, nc = grid3
    ns = ny * nx * nc
    T, D = q_ref.shape[1], q_ref.shape[2]
    H = D // HD
    DQ = D // Q
    FF = wg_ref.shape[2]
    nz = w_all.shape[0]
    rows_z = w_all.shape[1]
    PR = st_send.shape[1]
    RB = Q * slots
    groups = ns // GR
    GB = GR * RB
    GX = GR * slots
    n_exp = router_ref.shape[0]

    mz = lax.axis_index("dp")
    ms = lax.axis_index("seq")
    mc = ms % nc
    mx = (ms // nc) % nx
    my = ms // (nc * nx)
    right, left = (mz + 1) % nz, (mz + nz - 1) % nz

    def shifted(k, sign):
        dc, dx, dy = k % nc, (k // nc) % nx, k // (nc * nx)
        c = (mc + sign * dc + nc) % nc
        x = (mx + sign * dx + nx) % nx
        y = (my + sign * dy + ny) % ny
        return (y * nx + x) * nc + c

    barrier = pltpu.get_barrier_semaphore()

    def greet(k, carry):
        pl.semaphore_signal(barrier, inc=1, device_id={"seq": shifted(k, 1)}, device_id_type=MESH)
        return carry

    lax.fori_loop(1, ns, greet, 0)
    for z in (left, right):
        pl.semaphore_signal(barrier, inc=1, device_id={"dp": z}, device_id_type=MESH)

    w_all[mz, :, 0:FF] = wg_ref[0]
    w_all[mz, :, FF : 2 * FF] = wu_ref[0]
    w_all[mz, :, 2 * FF : 3 * FF] = wd_ref[0]

    for h in range(H):
        sl = slice(h * HD, (h + 1) * HD)
        state = dot(k_ref[0, :, sl], v_ref[0, :, sl], 0, 0).astype(BF16)
        n = HD // PR
        st_send[h * n : (h + 1) * n] = state.reshape(n, PR, HD)

    pl.semaphore_wait(barrier, ns - 1 + 2)

    n_right, n_left = nz // 2, nz - 1 - nz // 2
    piece = rows_z // SUB

    def ag_copy(way, s, u):
        chunk = (mz + nz - s) % nz if way == 0 else (mz + s) % nz
        ref = w_all.at[chunk, pl.ds(u * piece, piece), :]
        return pltpu.make_async_remote_copy(
            src_ref=ref,
            dst_ref=ref,
            send_sem=ag_ss.at[way, s, u],
            recv_sem=ag_rs.at[way, s, u],
            device_id={"dp": right if way == 0 else left},
            device_id_type=MESH,
        )

    def ag_wait(way, s, u):
        chunk = (mz + nz - 1 - s) % nz if way == 0 else (mz + 1 + s) % nz
        ref = w_all.at[chunk, pl.ds(u * piece, piece), :]
        pltpu.make_async_copy(ref, ref, ag_rs.at[way, s, u]).wait()

    def pump(s):
        for u in range(SUB):
            for way, count in ((0, n_right), (1, n_left)):
                if 1 <= s <= count:
                    ag_wait(way, s - 1, u)
                if s < count:
                    ag_copy(way, s, u).start()

    last = n_right
    done = [0]

    def pump_to(s):
        while done[0] <= min(s, last):
            pump(done[0])
            done[0] += 1

    pump_to(0)

    def send_states(src, dst, which):
        def one(k, carry):
            to = shifted(k, 1)
            pltpu.make_async_remote_copy(
                src_ref=src.at[to],
                dst_ref=dst.at[ms],
                send_sem=p_sem.at[which, 0],
                recv_sem=p_sem.at[which, 1],
                device_id={"seq": to},
                device_id_type=MESH,
            ).start()
            return carry

        lax.fori_loop(1, ns, one, 0)

    def wait_bytes(ref, sem):
        pltpu.make_async_copy(ref, ref, sem).wait()

    send_states(st_send, st_recv, 0)
    st_recv[ms] = st_send[ms]

    causal = lax.broadcasted_iota(jnp.int32, (T, T), 0) >= lax.broadcasted_iota(
        jnp.int32, (T, T), 1
    )
    for h in range(H):
        sl = slice(h * HD, (h + 1) * HD)
        scores = dot(q_ref[0, :, sl], k_ref[0, :, sl], 1, 1)
        wq[h, :, 0:T] = jnp.where(causal, scores, 0.0).astype(BF16)

    eye = lax.broadcasted_iota(jnp.int32, (T, T), 0) == lax.broadcasted_iota(jnp.int32, (T, T), 1)
    ids = ids_ref[0].astype(F32)

    def as_col(row):
        return jnp.sum(jnp.where(eye, row, 0.0), axis=1, keepdims=True)

    id0, id1 = as_col(ids[0:1]).astype(jnp.int32), as_col(ids[1:2]).astype(jnp.int32)
    lane_e = lax.broadcasted_iota(jnp.int32, (T, n_exp), 1)
    hot0, hot1 = (lane_e == id0).astype(F32), (lane_e == id1).astype(F32)
    below = (
        lax.broadcasted_iota(jnp.int32, (T, T), 0) > lax.broadcasted_iota(jnp.int32, (T, T), 1)
    ).astype(F32)
    counts = dot(below.astype(BF16), (hot0 + hot1).astype(BF16))

    def as_row(col):
        return jnp.sum(jnp.where(eye, col, 0.0), axis=0, keepdims=True)

    def relative(ident):
        c, x, y = ident % nc, (ident // nc) % nx, ident // (nc * nx)
        return (((y - my + ny) % ny) * nx + (x - mx + nx) % nx) * nc + (c - mc + nc) % nc

    rank0 = jnp.sum(counts * hot0, axis=1, keepdims=True)
    rank1 = jnp.sum(counts * hot1, axis=1, keepdims=True)
    rel_e = relative(lax.broadcasted_iota(jnp.int32, (1, n_exp), 1)).astype(F32)
    rel0 = jnp.sum(rel_e * hot0, axis=1, keepdims=True)
    rel1 = jnp.sum(rel_e * hot1, axis=1, keepdims=True)
    code0, code1 = rel0 * RB + rank0, rel1 * RB + rank1
    row0, row1 = as_row(code0).astype(jnp.int32), as_row(code1).astype(jnp.int32)
    icode0, icode1 = code0.astype(jnp.int32), code1.astype(jnp.int32)

    for q in range(Q):
        nst[q * T : (q + 1) * T, :] = cot_ref[0, :, q * DQ : (q + 1) * DQ]
    r_iota = lax.broadcasted_iota(jnp.int32, (GB, T), 0)
    for g in range(groups):
        for q in range(Q):
            at = r_iota + (g * GB - q * slots)
            hit = (at == row0) | (at == row1)
            place[g, :, q * T : (q + 1) * T] = jnp.where(hit, 1.0, 0.0).astype(BF16)

    def fill(g, buf):
        got = dot(place[g], nst[...]).astype(BF16)
        buf[pl.ds(g * GR, GR)] = got.reshape(GR, RB, DQ)

    def send_slot(k, src, dst, ss, rs, sign):
        return pltpu.make_async_remote_copy(
            src_ref=src.at[k],
            dst_ref=dst.at[k],
            send_sem=ss,
            recv_sem=rs,
            device_id={"seq": shifted(k, sign)},
            device_id_type=MESH,
        )

    def send_group(g, src, dst, ss, rs, sign):
        for i in range(GR):
            if g * GR + i > 0:
                send_slot(g * GR + i, src, dst, ss, rs.at[g], sign).start()

    def group_ref(g, buf):
        first = 1 if g == 0 else 0
        return buf.at[pl.ds(g * GR + first, GR - first)]

    for g in range(groups):
        fill(g, c_send)

    pump_to(1)
    wait_bytes(st_recv.at[pl.ds(0, ns - 1)], p_sem.at[0, 1])
    acc = jnp.zeros((PR, HD), F32)
    for j in range(ns):
        pf_send[j] = acc.astype(BF16)
        acc = acc + st_recv[j].astype(F32)
    send_states(pf_send, pf_recv, 1)
    pf_recv[ms] = pf_send[ms]

    for g in range(groups):
        send_group(g, c_send, c_recv, c_ss, c_rs, 1)
    c_recv[0] = c_send[0]
    pump_to(2)

    wait_bytes(pf_recv.at[pl.ds(0, ns - 1)], p_sem.at[1, 1])
    squares = jnp.zeros((T, HD), F32)
    for h in range(H):
        sl = slice(h * HD, (h + 1) * HD)
        n = HD // PR
        prefix = pf_recv[h * n : (h + 1) * n].reshape(HD, HD)
        att = dot(wq[h], v_ref[0, :, sl]) + dot(q_ref[0, :, sl], prefix)
        att = att * lax.rsqrt(jnp.mean(att * att, axis=-1, keepdims=True) + EPS)
        one = res_ref[0, :, sl].astype(F32) + att * again_ref[:, sl]
        stream[:, sl] = one
        squares = squares + one * one
    scale = lax.rsqrt(jnp.sum(squares, axis=-1, keepdims=True) / D + EPS)
    pump_to(3)
    logits = jnp.zeros((T, n_exp), F32)
    for q in range(Q):
        cols = slice(q * DQ, (q + 1) * DQ)
        part = (stream[:, cols] * scale * mgain_ref[:, cols]).astype(BF16)
        nst[q * T : (q + 1) * T, :] = part
        logits = logits + dot(part, router_ref[:, cols], 1, 1)

    for g in range(groups):
        fill(g, x_send)
        send_group(g, x_send, x_recv, x_ss, x_rs, 1)
    x_recv[0] = x_send[0]

    sig0 = jax.nn.sigmoid(jnp.sum(hot0 * logits, axis=1, keepdims=True))
    sig1 = jax.nn.sigmoid(jnp.sum(hot1 * logits, axis=1, keepdims=True))
    gate0, gate1 = sig0 / (sig0 + sig1), sig1 / (sig0 + sig1)
    low = lax.broadcasted_iota(jnp.int32, (T, 128), 1) >= 64

    def two_parts(gate):
        high = gate.astype(BF16).astype(F32)
        return jnp.where(low, gate - high, high).astype(BF16)

    g_rows = lax.broadcasted_iota(jnp.int32, (ns * 16, T), 0)
    grow0 = as_row(rel0 * 16 + rank0).astype(jnp.int32)
    grow1 = as_row(rel1 * 16 + rank1).astype(jnp.int32)
    g_msg = dot(jnp.where(g_rows == grow0, 1.0, 0.0).astype(BF16), two_parts(gate0)) + dot(
        jnp.where(g_rows == grow1, 1.0, 0.0).astype(BF16), two_parts(gate1)
    )
    g_send[...] = g_msg.astype(BF16).reshape(ns, 16, 128)

    def send_gate(k, carry):
        send_slot(k, g_send, g_recv, g_sem.at[0], g_sem.at[1], 1).start()
        return carry

    lax.fori_loop(1, ns, send_gate, 0)
    g_recv[0] = g_send[0]
    pump_to(4)

    l_iota = lax.broadcasted_iota(jnp.int32, (T, GB), 1)
    for g in range(groups):
        for q in range(Q):
            at = l_iota + (g * GB - q * slots)
            val = jnp.where(at == icode0, gate0, 0.0) + jnp.where(at == icode1, gate1, 0.0)
            placeg[q * T : (q + 1) * T, g * GB : (g + 1) * GB] = val.astype(BF16)
    pump_to(5)

    o = lax.broadcasted_iota(jnp.int32, (GB, GB), 0)
    c = lax.broadcasted_iota(jnp.int32, (GB, GB), 1)
    want = ((o // slots) % GR) * RB + (o // GX) * slots + o % slots
    perm = (c == want).astype(F32).astype(BF16)

    def unpack(g, src, dst):
        got = dot(perm, src[pl.ds(g * GR, GR)].reshape(GB, DQ)).astype(BF16)
        for q in range(Q):
            dst[g * GX : (g + 1) * GX, q * DQ : (q + 1) * DQ] = got[q * GX : (q + 1) * GX, :]

    for g in range(groups):
        wait_bytes(group_ref(g, c_recv), c_rs.at[g])
        unpack(g, c_recv, cs)
    pump_to(6)
    for g in range(groups):
        wait_bytes(group_ref(g, x_recv), x_rs.at[g])
        unpack(g, x_recv, xs)
        if g == groups // 2:
            pump_to(7)
    wait_bytes(g_recv.at[pl.ds(1, ns - 1)], g_sem.at[1])
    o16 = lax.broadcasted_iota(jnp.int32, (GX, GR * 16), 0)
    c16 = lax.broadcasted_iota(jnp.int32, (GX, GR * 16), 1)
    pick = (c16 == (o16 // slots) * 16 + o16 % slots).astype(F32).astype(BF16)
    for g in range(groups):
        got = dot(pick, g_recv[pl.ds(g * GR, GR)].reshape(GR * 16, 128))
        gcol[g * GX : (g + 1) * GX, :] = got[:, 0:1] + got[:, 64:65]
    pump_to(last)

    KB = rows_z * 2

    def fwd(i, carry):
        cols = pl.ds(pl.multiple_of(i * KB, KB), KB)
        w = w_all[pl.ds(2 * i, 2)].reshape(KB, 3 * FF)
        pre[:, 0 : 2 * FF] += dot(xs[:, cols], w[:, 0 : 2 * FF])
        pre[:, 2 * FF : 3 * FF] += dot(cs[:, cols], w[:, 2 * FF : 3 * FF])
        return carry

    pre[...] = jnp.zeros_like(pre)
    lax.fori_loop(0, nz // 2, fwd, 0)
    pre_gate = pre[:, 0:FF]
    pre_up = pre[:, FF : 2 * FF]
    gates = gcol[...]
    d_hidden = pre[:, 2 * FF : 3 * FF] * gates
    sigma = jax.nn.sigmoid(pre_gate)
    act = pre_gate * sigma
    hidden = (act * pre_up).astype(BF16)
    hid[...] = hidden
    hidg[...] = (hidden.astype(F32) * gates).astype(BF16)
    dgu[:, 0:FF] = (d_hidden * pre_up * sigma * (1.0 + pre_gate * (1.0 - sigma))).astype(BF16)
    dgu[:, FF : 2 * FF] = (d_hidden * act).astype(BF16)

    half = rows_z // SUB

    def grad_of(chunk):
        cols = pl.ds(pl.multiple_of(chunk * rows_z, rows_z), rows_z)
        return dot(xs[:, cols], dgu[...], 0, 0), dot(cs[:, cols], hidg[...], 0, 0)

    def rs_copy(way, s, u):
        return pltpu.make_async_remote_copy(
            src_ref=rs_send.at[way, s, pl.ds(u * half, half)],
            dst_ref=rs_recv.at[way, s, pl.ds(u * half, half)],
            send_sem=rr_ss.at[way, s, u],
            recv_sem=rr_rs.at[way, s, u],
            device_id={"dp": right if way == 0 else left},
            device_id_type=MESH,
        )

    def rs_step(s):
        for way, count in ((0, n_right), (1, n_left)):
            if s >= count:
                continue
            chunk = (mz + n_right - s) % nz if way == 0 else (mz + nz - n_left + s) % nz
            a, b = grad_of(chunk)
            for u in range(SUB):
                rows = slice(u * half, (u + 1) * half)
                pa, pb = a[rows], b[rows]
                if s > 0:
                    rs_copy(way, s - 1, u).wait_recv()
                    pa = pa + rs_recv[way, s - 1, rows, 0 : 2 * FF].astype(F32)
                    pb = pb + rs_recv[way, s - 1, rows, 2 * FF : 3 * FF].astype(F32)
                rs_send[way, s, rows, 0 : 2 * FF] = pa.astype(BF16)
                rs_send[way, s, rows, 2 * FF : 3 * FF] = pb.astype(BF16)
                rs_copy(way, s, u).start()

    rs_step(0)

    for g in range(groups):
        h_g = hid[g * GX : (g + 1) * GX, :]
        parts = []
        for q in range(Q):
            n = nz // Q
            w_q = w_all[q * n : (q + 1) * n, :, 2 * FF : 3 * FF].reshape(DQ, FF)
            parts.append(dot(h_g, w_q, 1, 1).astype(BF16))
        stacked = jnp.concatenate(parts, axis=0)
        r_send[pl.ds(g * GR, GR)] = dot(perm, stacked, 0, 0).astype(BF16).reshape(GR, RB, DQ)
        send_group(g, r_send, r_recv, r_ss, r_rs, -1)
    r_recv[0] = r_send[0]

    for s in range(1, n_right):
        rs_step(s)
        if s == n_right // 2 + 1 or n_right < 4:
            if s == n_right // 2 + 1 or s == n_right - 1:
                for g in range(groups):
                    wait_bytes(group_ref(g, r_recv), r_rs.at[g])
                back = r_recv[...].reshape(ns * RB, DQ)
                for q in range(Q):
                    cols = slice(q * DQ, (q + 1) * DQ)
                    got = dot(placeg[q * T : (q + 1) * T, :], back)
                    mixed_ref[0, :, cols] = (stream[:, cols] + got).astype(BF16)

    a, b = grad_of(mz)
    flag = (train_ref[0] > 0).astype(F32)
    for u in range(SUB):
        rows = slice(u * half, (u + 1) * half)
        pa, pb = a[rows], b[rows]
        for way, count in ((1, n_left), (0, n_right)):
            rs_copy(way, count - 1, u).wait_recv()
            pa = pa + rs_recv[way, count - 1, rows, 0 : 2 * FF].astype(F32)
            pb = pb + rs_recv[way, count - 1, rows, 2 * FF : 3 * FF].astype(F32)
        gg_ref[0, rows, :] = pa[:, 0:FF] * flag
        gu_ref[0, rows, :] = pa[:, FF : 2 * FF] * flag
        gd_ref[0, rows, :] = pb * flag

    for way, count in ((0, n_right), (1, n_left)):
        for s in range(count):
            for u in range(SUB):
                ag_copy(way, s, u).wait_send()
                rs_copy(way, s, u).wait_send()
    for which in range(2):
        wait_bytes(st_send.at[pl.ds(0, ns - 1)], p_sem.at[which, 0])
    wait_bytes(c_send.at[pl.ds(1, ns - 1)], c_ss)
    wait_bytes(x_send.at[pl.ds(1, ns - 1)], x_ss)
    wait_bytes(g_send.at[pl.ds(1, ns - 1)], g_sem.at[0])
    wait_bytes(r_send.at[pl.ds(1, ns - 1)], r_ss)


def body(
    grid3,
    nz,
    queries,
    keys,
    values,
    residual_in,
    cotangent,
    expert_ids,
    router,
    attn_gain,
    moe_gain,
    w_gate,
    w_up,
    w_down,
    trainable,
):
    ns = grid3[0] * grid3[1] * grid3[2]
    T, D = queries.shape[1:]
    H = D // HD
    FF = w_gate.shape[2]
    slots = max(2, 3 * T // ns)
    rows_z = w_gate.shape[1]
    RB, DQ, R = Q * slots, D // Q, ns * slots
    PR = H * HD // ns
    groups = ns // GR
    n_right = nz // 2
    vm = pltpu.VMEM
    dma = pltpu.SemaphoreType.DMA
    scratch = [
        vm((nz, rows_z, 3 * FF), BF16),
        vm((ns, PR, HD), BF16),
        vm((ns, PR, HD), BF16),
        vm((ns, PR, HD), BF16),
        vm((ns, PR, HD), BF16),
        vm((H, T, T), BF16),
        vm((T, D), F32),
        vm((Q * T, DQ), BF16),
        vm((groups, GR * RB, Q * T), BF16),
        vm((Q * T, ns * RB), BF16),
        vm((ns, RB, DQ), BF16),
        vm((ns, RB, DQ), BF16),
        vm((ns, RB, DQ), BF16),
        vm((ns, RB, DQ), BF16),
        vm((ns, 16, 128), BF16),
        vm((ns, 16, 128), BF16),
        vm((R, D), BF16),
        vm((R, D), BF16),
        vm((R, 3 * FF), F32),
        vm((R, 1), F32),
        vm((R, 2 * FF), BF16),
        vm((R, FF), BF16),
        vm((R, FF), BF16),
        vm((ns, RB, DQ), BF16),
        vm((ns, RB, DQ), BF16),
        vm((2, n_right, rows_z, 3 * FF), BF16),
        vm((2, n_right, rows_z, 3 * FF), BF16),
        dma((2, n_right, SUB)),
        dma((2, n_right, SUB)),
        dma((2, 2)),
        dma(()),
        dma((groups,)),
        dma(()),
        dma((groups,)),
        dma((2,)),
        dma(()),
        dma((groups,)),
        dma((2, n_right, SUB)),
        dma((2, n_right, SUB)),
    ]
    in_vmem = pl.BlockSpec(memory_space=pltpu.VMEM)
    return pl.pallas_call(
        functools.partial(kernel, grid3, slots),
        out_shape=(
            jax.ShapeDtypeStruct((1, T, D), BF16),
            jax.ShapeDtypeStruct((1, rows_z, FF), F32),
            jax.ShapeDtypeStruct((1, rows_z, FF), F32),
            jax.ShapeDtypeStruct((1, rows_z, FF), F32),
        ),
        in_specs=[in_vmem] * 12 + [pl.BlockSpec(memory_space=pltpu.SMEM)],
        out_specs=(in_vmem,) * 4,
        scratch_shapes=scratch,
        compiler_params=pltpu.CompilerParams(
            collective_id=0, has_side_effects=True, vmem_limit_bytes=60 * 1024 * 1024
        ),
        name="layer",
    )(
        queries,
        keys,
        values,
        residual_in,
        cotangent,
        jnp.transpose(expert_ids, (0, 2, 1)),
        router.T,
        attn_gain.reshape(1, D),
        moe_gain.reshape(1, D),
        w_gate,
        w_up,
        w_down,
        trainable,
    )


def solution(mesh, grid3=(4, 4, 2)):
    blocks = P("dp", "seq", None)
    weights = P("seq", "dp", None)
    return jax.shard_map(
        functools.partial(body, grid3, mesh.shape["dp"]),
        mesh=mesh,
        in_specs=(blocks,) * 6 + (P(), P(), P()) + (weights,) * 3 + (P("seq"),),
        out_specs=(blocks, weights, weights, weights),
        check_vma=False,
    )
```

```python
import functools

import jax
import jax.numpy as jnp
from jax import lax
from jax.experimental import pallas as pl
from jax.experimental.pallas import tpu as pltpu
from jax.sharding import PartitionSpec as P

HD = 128
EPS = 1e-06
MESH = pl.DeviceIdType.MESH
F32 = jnp.float32
BF16 = jnp.bfloat16
Q = 4
GR = 4
SUB = 2


def early(groups):
    return [[g for g in range(groups) if min(g * 8 // groups, 7) in at] for at in ((0,), (1, 2), (3, 4), (5, 6, 7))]


def dot(a, b, ca=1, cb=0):
    return lax.dot_general(a, b, (((ca,), (cb,)), ((), ())), preferred_element_type=F32)


def kernel(
    grid3,
    slots,
    q_in,
    k_in,
    v_in,
    res_in,
    cot_in,
    ids_ref,
    router_ref,
    again_ref,
    mgain_ref,
    wg_in,
    wu_in,
    wd_in,
    train_ref,
    mixed_ref,
    gg_ref,
    gu_ref,
    gd_ref,
    in_sem,
    q_ref,
    k_ref,
    v_ref,
    res_ref,
    cot_ref,
    w_all,
    st,
    sib,
    cs_send,
    cs_recv,
    pf_send,
    pf_recv,
    up_send,
    pfx,
    wq,
    stream,
    nst,
    place,
    placeg,
    c_send,
    c_recv,
    x_send,
    x_recv,
    g_send,
    g_recv,
    xs,
    cs,
    pre,
    gcol,
    dgu,
    hid,
    hidg,
    r_send,
    r_recv,
    gbuf,
    rs_send,
    rs_recv,
    ag_ss,
    ag_rs,
    p_sem,
    c_ss,
    c_rs,
    x_ss,
    x_rs,
    g_sem,
    r_ss,
    r_rs,
    rr_ss,
    rr_rs,
):
    ny, nx, nc = grid3
    ns = ny * nx * nc
    T, D = q_ref.shape
    H = D // HD
    DQ = D // Q
    FF = wg_in.shape[2]
    nz = w_all.shape[0]
    rows_z = w_all.shape[1]
    chips, PR = st.shape[1], st.shape[2]
    RB = Q * slots
    groups = ns // GR
    GB = GR * RB
    GX = GR * slots
    n_exp = router_ref.shape[0]

    mz = lax.axis_index("dp")
    ms = lax.axis_index("seq")
    mc = ms % nc
    mx = (ms // nc) % nx
    my = ms // (nc * nx)
    right, left = (mz + 1) % nz, (mz + nz - 1) % nz

    mchip = my * nx + mx

    def hops(p):
        dx, dy = (p // nc) % nx, p // (nc * nx)
        return min(dx, nx - dx) + min(dy, ny - dy)

    slot_list = [0] + sorted(range(1, ns), key=lambda p: -hops(p))

    def moved(p, sign):
        dc, dx, dy = p % nc, (p // nc) % nx, p // (nc * nx)
        c = (mc + sign * dc + nc) % nc
        x = (mx + sign * dx + nx) % nx
        y = (my + sign * dy + ny) % ny
        return (y * nx + x) * nc + c

    def shifted(k, sign):
        return moved(slot_list[k], sign)

    loads = {}
    for n, (name, src, dst) in enumerate(
        (
            ("k", k_in.at[0], k_ref),
            ("v", v_in.at[0], v_ref),
            ("gate", wg_in.at[0], w_all.at[mz, :, pl.ds(0, FF)]),
            ("up", wu_in.at[0], w_all.at[mz, :, pl.ds(FF, FF)]),
            ("down", wd_in.at[0], w_all.at[mz, :, pl.ds(2 * FF, FF)]),
            ("cot", cot_in.at[0], cot_ref),
            ("q", q_in.at[0], q_ref),
            ("res", res_in.at[0], res_ref),
        )
    ):
        loads[name] = pltpu.make_async_copy(src, dst, in_sem.at[n])
        loads[name].start()

    barrier = pltpu.get_barrier_semaphore()

    def greet(k, carry):
        pl.semaphore_signal(barrier, inc=1, device_id={"seq": moved(k, 1)}, device_id_type=MESH)
        return carry

    lax.fori_loop(1, ns, greet, 0)
    for z in (left, right):
        pl.semaphore_signal(barrier, inc=1, device_id={"dp": z}, device_id_type=MESH)

    for name in ("gate", "up", "down"):
        loads[name].wait()

    steps = nz // 2
    piece = rows_z // SUB
    near = (right, left)

    def order(way):
        return range(SUB) if way == 0 else range(SUB - 1, -1, -1)

    def far_half(way, u):
        return (u < SUB // 2) == (way == 0)

    def ag_copy(way, s, u):
        chunk = (mz + nz - s) % nz if way == 0 else (mz + s) % nz
        ref = w_all.at[chunk, pl.ds(u * piece, piece), :]
        return pltpu.make_async_remote_copy(
            src_ref=ref,
            dst_ref=ref,
            send_sem=ag_ss.at[way, s, u],
            recv_sem=ag_rs.at[way, s, u],
            device_id={"dp": near[way]},
            device_id_type=MESH,
        )

    def ag_wait(way, s, u):
        chunk = (mz + nz - 1 - s) % nz if way == 0 else (mz + 1 + s) % nz
        ref = w_all.at[chunk, pl.ds(u * piece, piece), :]
        pltpu.make_async_copy(ref, ref, ag_rs.at[way, s, u]).wait()

    def ag_used(way, s, u):
        return 0 <= s < steps and (s < steps - 1 or far_half(way, u))

    def pump(s, i):
        for way in (0, 1):
            u = order(way)[i]
            if ag_used(way, s - 1, u):
                ag_wait(way, s - 1, u)
            if ag_used(way, s, u):
                ag_copy(way, s, u).start()

    items = [(s, i) for s in range(steps + 1) for i in range(SUB)]

    def pump_to(s, i=SUB - 1):
        while items and items[0] <= (s, i):
            pump(*items.pop(0))

    loads["k"].wait()
    loads["v"].wait()
    n_piece = HD // PR
    for h in range(H):
        sl = slice(h * HD, (h + 1) * HD)
        state = dot(k_ref[:, sl], v_ref[:, sl], 0, 0).astype(BF16)
        for i in range(n_piece):
            p = h * n_piece + i
            st[p % nc, p // nc] = state[i * PR : (i + 1) * PR, :]

    pl.semaphore_wait(barrier, ns - 1 + 2)
    pump_to(0)

    sibling = mchip * nc + (1 - mc)
    pair_a = pltpu.make_async_remote_copy(
        src_ref=st.at[1 - mc],
        dst_ref=sib,
        send_sem=p_sem.at[0, 0],
        recv_sem=p_sem.at[0, 1],
        device_id={"seq": sibling},
        device_id_type=MESH,
    )
    pair_a.start()

    def wait_bytes(ref, sem):
        pltpu.make_async_copy(ref, ref, sem).wait()

    def send_pieces(src, dst, which):
        for p in sorted(range(1, chips), key=lambda p: -hops(p * nc)):
            to = moved(p * nc, 1)
            pltpu.make_async_remote_copy(
                src_ref=src.at[to // nc],
                dst_ref=dst.at[mchip],
                send_sem=p_sem.at[which, 0],
                recv_sem=p_sem.at[which, 1],
                device_id={"seq": to},
                device_id_type=MESH,
            ).start()

    eye = lax.broadcasted_iota(jnp.int32, (T, T), 0) == lax.broadcasted_iota(jnp.int32, (T, T), 1)
    ids = ids_ref[0].astype(F32)

    def as_col(row):
        return jnp.sum(jnp.where(eye, row, 0.0), axis=1, keepdims=True)

    id0, id1 = as_col(ids[0:1]).astype(jnp.int32), as_col(ids[1:2]).astype(jnp.int32)
    lane_e = lax.broadcasted_iota(jnp.int32, (T, n_exp), 1)
    hot0, hot1 = (lane_e == id0).astype(F32), (lane_e == id1).astype(F32)
    below = (
        lax.broadcasted_iota(jnp.int32, (T, T), 0) > lax.broadcasted_iota(jnp.int32, (T, T), 1)
    ).astype(F32)
    counts = dot(below.astype(BF16), (hot0 + hot1).astype(BF16))

    def as_row(col):
        return jnp.sum(jnp.where(eye, col, 0.0), axis=0, keepdims=True)

    def relative(ident):
        c, x, y = ident % nc, (ident // nc) % nx, ident // (nc * nx)
        return (((y - my + ny) % ny) * nx + (x - mx + nx) % nx) * nc + (c - mc + nc) % nc

    rank0 = jnp.sum(counts * hot0, axis=1, keepdims=True)
    rank1 = jnp.sum(counts * hot1, axis=1, keepdims=True)
    rel_n = relative(lax.broadcasted_iota(jnp.int32, (1, n_exp), 1))
    rel_e = jnp.zeros((1, n_exp), F32)
    for k in range(1, ns):
        rel_e = rel_e + jnp.where(rel_n == slot_list[k], float(k), 0.0)
    rel0 = jnp.sum(rel_e * hot0, axis=1, keepdims=True)
    rel1 = jnp.sum(rel_e * hot1, axis=1, keepdims=True)
    code0, code1 = rel0 * RB + rank0, rel1 * RB + rank1
    row0, row1 = as_row(code0).astype(jnp.int32), as_row(code1).astype(jnp.int32)
    icode0, icode1 = code0.astype(jnp.int32), code1.astype(jnp.int32)

    loads["cot"].wait()
    for q in range(Q):
        nst[q * T : (q + 1) * T, :] = cot_ref[:, q * DQ : (q + 1) * DQ]
    r_iota = lax.broadcasted_iota(jnp.int32, (GB, T), 0)
    for g in range(groups):
        for q in range(Q):
            at = r_iota + (g * GB - q * slots)
            hit = (at == row0) | (at == row1)
            place[g, :, q * T : (q + 1) * T] = jnp.where(hit, 1.0, 0.0).astype(BF16)

    pair_a.wait_recv()
    cs_send[...] = (st[mc].astype(F32) + sib[...].astype(F32)).astype(BF16)

    send_pieces(cs_send, cs_recv, 1)
    cs_recv[mchip] = cs_send[mchip]
    def fill(g, buf):
        got = dot(place[g], nst[...]).astype(BF16)
        buf[pl.ds(g * GR, GR)] = got.reshape(GR, RB, DQ)

    def send_slot(k, src, dst, ss, rs, sign):
        return pltpu.make_async_remote_copy(
            src_ref=src.at[k],
            dst_ref=dst.at[k],
            send_sem=ss,
            recv_sem=rs,
            device_id={"seq": shifted(k, sign)},
            device_id_type=MESH,
        )

    def send_group(g, src, dst, ss, rs, sign):
        for i in range(GR):
            if g * GR + i > 0:
                send_slot(g * GR + i, src, dst, ss, rs.at[g], sign).start()

    def group_ref(g, buf):
        first = 1 if g == 0 else 0
        return buf.at[pl.ds(g * GR + first, GR - first)]

    for g in range(groups):
        fill(g, c_send)
        if g in early(groups)[0]:
            send_group(g, c_send, c_recv, c_ss, c_rs, 1)
    pump_to(1, 0)
    for g in early(groups)[1]:
        send_group(g, c_send, c_recv, c_ss, c_rs, 1)

    loads["q"].wait()
    loads["res"].wait()
    causal = lax.broadcasted_iota(jnp.int32, (T, T), 0) >= lax.broadcasted_iota(
        jnp.int32, (T, T), 1
    )
    for h in range(H):
        sl = slice(h * HD, (h + 1) * HD)
        scores = dot(q_ref[:, sl], k_ref[:, sl], 1, 1)
        wq[h, :, 0:T] = jnp.where(causal, scores, 0.0).astype(BF16)

    pump_to(1)
    wait_bytes(cs_recv.at[pl.ds(0, chips - 1)], p_sem.at[1, 1])
    acc = jnp.zeros((PR, HD), F32)
    for j in range(chips):
        pf_send[j] = acc.astype(BF16)
        acc = acc + cs_recv[j].astype(F32)
    send_pieces(pf_send, pf_recv, 2)
    pf_recv[mchip] = pf_send[mchip]
    pump_to(2, 0)
    for g in early(groups)[2]:
        send_group(g, c_send, c_recv, c_ss, c_rs, 1)
    pump_to(2)

    second = mc.astype(F32)
    wait_bytes(pf_recv.at[pl.ds(0, chips - 1)], p_sem.at[2, 1])
    got = pf_recv[...].astype(F32)
    up_send[...] = (got + (1.0 - second) * st[mc].astype(F32)).astype(BF16)
    pair_b = pltpu.make_async_remote_copy(
        src_ref=up_send,
        dst_ref=pfx.at[mc],
        send_sem=p_sem.at[3, 0],
        recv_sem=p_sem.at[3, 1],
        device_id={"seq": sibling},
        device_id_type=MESH,
    )
    pair_b.start()
    pfx[mc] = (got + second * sib[...].astype(F32)).astype(BF16)
    for g in early(groups)[3]:
        send_group(g, c_send, c_recv, c_ss, c_rs, 1)
    c_recv[0] = c_send[0]
    pump_to(3, 0)
    pair_b.wait_recv()

    squares = jnp.zeros((T, HD), F32)
    for h in range(H):
        sl = slice(h * HD, (h + 1) * HD)
        ps = range(h * n_piece, (h + 1) * n_piece)
        prefix = jnp.concatenate([pfx[p % nc, p // nc] for p in ps], axis=0)
        att = dot(wq[h], v_ref[:, sl]) + dot(q_ref[:, sl], prefix)
        att = att * lax.rsqrt(jnp.mean(att * att, axis=-1, keepdims=True) + EPS)
        one = res_ref[:, sl].astype(F32) + att * again_ref[:, sl]
        stream[:, sl] = one
        squares = squares + one * one
        if h == H // 2:
            pump_to(3)
    scale = lax.rsqrt(jnp.sum(squares, axis=-1, keepdims=True) / D + EPS)
    logits = jnp.zeros((T, n_exp), F32)
    for q in range(Q):
        cols = slice(q * DQ, (q + 1) * DQ)
        part = (stream[:, cols] * scale * mgain_ref[:, cols]).astype(BF16)
        nst[q * T : (q + 1) * T, :] = part
        logits = logits + dot(part, router_ref[:, cols], 1, 1)
    pump_to(4, 0)

    for g in range(groups):
        fill(g, x_send)
        send_group(g, x_send, x_recv, x_ss, x_rs, 1)
    pump_to(4)
    x_recv[0] = x_send[0]

    sig0 = jax.nn.sigmoid(jnp.sum(hot0 * logits, axis=1, keepdims=True))
    sig1 = jax.nn.sigmoid(jnp.sum(hot1 * logits, axis=1, keepdims=True))
    gate0, gate1 = sig0 / (sig0 + sig1), sig1 / (sig0 + sig1)
    low = lax.broadcasted_iota(jnp.int32, (T, 128), 1) >= 64

    def two_parts(gate):
        high = gate.astype(BF16).astype(F32)
        return jnp.where(low, gate - high, high).astype(BF16)

    g_rows = lax.broadcasted_iota(jnp.int32, (ns * 16, T), 0)
    grow0 = as_row(rel0 * 16 + rank0).astype(jnp.int32)
    grow1 = as_row(rel1 * 16 + rank1).astype(jnp.int32)
    g_msg = dot(jnp.where(g_rows == grow0, 1.0, 0.0).astype(BF16), two_parts(gate0)) + dot(
        jnp.where(g_rows == grow1, 1.0, 0.0).astype(BF16), two_parts(gate1)
    )
    g_send[...] = g_msg.astype(BF16).reshape(ns, 16, 128)

    for k in range(1, ns):
        send_slot(k, g_send, g_recv, g_sem.at[0], g_sem.at[1], 1).start()
    g_recv[0] = g_send[0]
    pump_to(5, 0)

    l_iota = lax.broadcasted_iota(jnp.int32, (T, GB), 1)
    for g in range(groups):
        for q in range(Q):
            at = l_iota + (g * GB - q * slots)
            val = jnp.where(at == icode0, gate0, 0.0) + jnp.where(at == icode1, gate1, 0.0)
            placeg[q * T : (q + 1) * T, g * GB : (g + 1) * GB] = val.astype(BF16)
    pump_to(5)

    o = lax.broadcasted_iota(jnp.int32, (GB, GB), 0)
    c = lax.broadcasted_iota(jnp.int32, (GB, GB), 1)
    want = ((o // slots) % GR) * RB + (o // GX) * slots + o % slots
    perm = (c == want).astype(F32).astype(BF16)

    def unpack(g, src, dst):
        got = dot(perm, src[pl.ds(g * GR, GR)].reshape(GB, DQ)).astype(BF16)
        for q in range(Q):
            dst[g * GX : (g + 1) * GX, q * DQ : (q + 1) * DQ] = got[q * GX : (q + 1) * GX, :]

    KB = rows_z * 2

    def matmul_rows(src, rows, c0, c1):
        def one(i, carry):
            cols = pl.ds(pl.multiple_of(i * KB, KB), KB)
            w = w_all[pl.ds(2 * i, 2), :, c0:c1].reshape(KB, c1 - c0)
            pre[rows, c0:c1] += dot(src[rows, cols], w)
            return carry

        lax.fori_loop(0, nz // 2, one, 0)

    pre[...] = jnp.zeros_like(pre)
    for g in range(groups):
        wait_bytes(group_ref(g, c_recv), c_rs.at[g])
        unpack(g, c_recv, cs)
        if g == groups // 2:
            pump_to(6, 0)
    pump_to(6)
    first_half = groups // 2
    for g in range(first_half):
        wait_bytes(group_ref(g, x_recv), x_rs.at[g])
        unpack(g, x_recv, xs)
        if g == 0:
            pump_to(7, 0)
        elif g == first_half // 2:
            pump_to(7)
    pump_to(steps)
    cut = first_half * GX
    R = ns * slots
    matmul_rows(cs, slice(0, R), 2 * FF, 3 * FF)
    if cut:
        matmul_rows(xs, slice(0, cut), 0, 2 * FF)
    for g in range(first_half, groups):
        wait_bytes(group_ref(g, x_recv), x_rs.at[g])
        unpack(g, x_recv, xs)
    matmul_rows(xs, slice(cut, R), 0, 2 * FF)
    wait_bytes(g_recv.at[pl.ds(1, ns - 1)], g_sem.at[1])
    o16 = lax.broadcasted_iota(jnp.int32, (GX, GR * 16), 0)
    c16 = lax.broadcasted_iota(jnp.int32, (GX, GR * 16), 1)
    pick = (c16 == (o16 // slots) * 16 + o16 % slots).astype(F32).astype(BF16)
    for g in range(groups):
        got = dot(pick, g_recv[pl.ds(g * GR, GR)].reshape(GR * 16, 128))
        gcol[g * GX : (g + 1) * GX, :] = got[:, 0:1] + got[:, 64:65]

    pre_gate = pre[:, 0:FF]
    pre_up = pre[:, FF : 2 * FF]
    gates = gcol[...]
    d_hidden = pre[:, 2 * FF : 3 * FF] * gates
    sigma = jax.nn.sigmoid(pre_gate)
    act = pre_gate * sigma
    hidden = (act * pre_up).astype(BF16)
    hid[...] = hidden
    hidg[...] = (hidden.astype(F32) * gates).astype(BF16)
    dgu[:, 0:FF] = (d_hidden * pre_up * sigma * (1.0 + pre_gate * (1.0 - sigma))).astype(BF16)
    dgu[:, FF : 2 * FF] = (d_hidden * act).astype(BF16)

    half = rows_z // SUB

    def grad_of(chunk):
        cols = pl.ds(pl.multiple_of(chunk * rows_z, rows_z), rows_z)
        return dot(xs[:, cols], dgu[...], 0, 0), dot(cs[:, cols], hidg[...], 0, 0)

    def rs_copy(way, s, u):
        return pltpu.make_async_remote_copy(
            src_ref=rs_send.at[way, s, pl.ds(u * half, half)],
            dst_ref=rs_recv.at[way, s, pl.ds(u * half, half)],
            send_sem=rr_ss.at[way, s, u],
            recv_sem=rr_rs.at[way, s, u],
            device_id={"dp": near[way]},
            device_id_type=MESH,
        )

    def rs_used(way, s, u):
        return 0 <= s < steps and (s > 0 or far_half(way, u))

    def rs_order(way):
        return range(SUB - 1, -1, -1) if way == 0 else range(SUB)

    def rs_grads(s):
        for way in (0, 1):
            if way == 1 and s == 0:
                continue
            chunk = (mz + steps - s) % nz if way == 0 else (mz + nz - steps + s) % nz
            a, b = grad_of(chunk)
            gbuf[way, :, 0 : 2 * FF] = a
            gbuf[way, :, 2 * FF : 3 * FF] = b

    def rs_piece(way, s, u):
        rows = slice(u * half, (u + 1) * half)
        val = gbuf[0 if s == 0 else way, rows, :]
        if rs_used(way, s - 1, u):
            rs_copy(way, s - 1, u).wait_recv()
            val = val + rs_recv[way, s - 1, rows, :].astype(F32)
        rs_send[way, s, rows, :] = val.astype(BF16)
        rs_copy(way, s, u).start()

    def rs_pieces(s, when):
        for i in range(SUB):
            for way in (0, 1):
                u = rs_order(way)[i]
                if rs_used(way, s, u) and when(rs_used(way, s - 1, u)):
                    rs_piece(way, s, u)

    def always(waits):
        return True

    rs_grads(0)
    rs_pieces(0, always)
    rs_grads(1)
    rs_pieces(1, lambda waits: not waits)

    for g in range(groups):
        h_g = hid[g * GX : (g + 1) * GX, :]
        parts = []
        for q in range(Q):
            n = nz // Q
            w_q = w_all[q * n : (q + 1) * n, :, 2 * FF : 3 * FF].reshape(DQ, FF)
            parts.append(dot(h_g, w_q, 1, 1).astype(BF16))
        stacked = jnp.concatenate(parts, axis=0)
        r_send[pl.ds(g * GR, GR)] = dot(perm, stacked, 0, 0).astype(BF16).reshape(GR, RB, DQ)
        send_group(g, r_send, r_recv, r_ss, r_rs, -1)
    r_recv[0] = r_send[0]

    rs_pieces(1, lambda waits: waits)

    for s in range(2, steps + 1):
        if s < steps:
            rs_grads(s)
            rs_pieces(s, always)
        if s == (5 if steps > 5 else steps):
            for g in range(groups):
                wait_bytes(group_ref(g, r_recv), r_rs.at[g])
            back = r_recv[...].reshape(ns * RB, DQ)
            for q in range(Q):
                cols = slice(q * DQ, (q + 1) * DQ)
                got = dot(placeg[q * T : (q + 1) * T, :], back)
                mixed_ref[0, :, cols] = (stream[:, cols] + got).astype(BF16)

    a, b = grad_of(mz)
    gbuf[0, :, 0 : 2 * FF] = a
    gbuf[0, :, 2 * FF : 3 * FF] = b
    flag = (train_ref[0] > 0).astype(F32)
    for way in (0, 1):
        for u in rs_order(way):
            rows = slice(u * half, (u + 1) * half)
            rs_copy(way, steps - 1, u).wait_recv()
            gbuf[0, rows, :] = gbuf[0, rows, :] + rs_recv[way, steps - 1, rows, :].astype(F32)
    gg_ref[0] = gbuf[0, :, 0:FF] * flag
    gu_ref[0] = gbuf[0, :, FF : 2 * FF] * flag
    gd_ref[0] = gbuf[0, :, 2 * FF : 3 * FF] * flag

    for way in (0, 1):
        for s in range(steps):
            for u in range(SUB):
                if ag_used(way, s, u):
                    ag_copy(way, s, u).wait_send()
                if rs_used(way, s, u):
                    rs_copy(way, s, u).wait_send()
    pair_a.wait_send()
    pair_b.wait_send()
    wait_bytes(cs_send.at[pl.ds(0, chips - 1)], p_sem.at[1, 0])
    wait_bytes(pf_send.at[pl.ds(0, chips - 1)], p_sem.at[2, 0])
    wait_bytes(c_send.at[pl.ds(1, ns - 1)], c_ss)
    wait_bytes(x_send.at[pl.ds(1, ns - 1)], x_ss)
    wait_bytes(g_send.at[pl.ds(1, ns - 1)], g_sem.at[0])
    wait_bytes(r_send.at[pl.ds(1, ns - 1)], r_ss)


def body(
    grid3,
    nz,
    queries,
    keys,
    values,
    residual_in,
    cotangent,
    expert_ids,
    router,
    attn_gain,
    moe_gain,
    w_gate,
    w_up,
    w_down,
    trainable,
):
    ns = grid3[0] * grid3[1] * grid3[2]
    T, D = queries.shape[1:]
    H = D // HD
    FF = w_gate.shape[2]
    slots = max(2, 3 * T // ns)
    rows_z = w_gate.shape[1]
    RB, DQ, R = Q * slots, D // Q, ns * slots
    PR = H * HD // ns
    groups = ns // GR
    steps = nz // 2
    nc = grid3[2]
    chips = ns // nc
    vm = pltpu.VMEM
    dma = pltpu.SemaphoreType.DMA
    scratch = [
        dma((8,)),
        vm((T, D), BF16),
        vm((T, D), BF16),
        vm((T, D), BF16),
        vm((T, D), BF16),
        vm((T, D), BF16),
        vm((nz, rows_z, 3 * FF), BF16),
        vm((nc, chips, PR, HD), BF16),
        vm((chips, PR, HD), BF16),
        vm((chips, PR, HD), BF16),
        vm((chips, PR, HD), BF16),
        vm((chips, PR, HD), BF16),
        vm((chips, PR, HD), BF16),
        vm((chips, PR, HD), BF16),
        vm((nc, chips, PR, HD), BF16),
        vm((H, T, T), BF16),
        vm((T, D), F32),
        vm((Q * T, DQ), BF16),
        vm((groups, GR * RB, Q * T), BF16),
        vm((Q * T, ns * RB), BF16),
        vm((ns, RB, DQ), BF16),
        vm((ns, RB, DQ), BF16),
        vm((ns, RB, DQ), BF16),
        vm((ns, RB, DQ), BF16),
        vm((ns, 16, 128), BF16),
        vm((ns, 16, 128), BF16),
        vm((R, D), BF16),
        vm((R, D), BF16),
        vm((R, 3 * FF), F32),
        vm((R, 1), F32),
        vm((R, 2 * FF), BF16),
        vm((R, FF), BF16),
        vm((R, FF), BF16),
        vm((ns, RB, DQ), BF16),
        vm((ns, RB, DQ), BF16),
        vm((2, rows_z, 3 * FF), F32),
        vm((2, steps, rows_z, 3 * FF), BF16),
        vm((2, steps, rows_z, 3 * FF), BF16),
        dma((2, steps, SUB)),
        dma((2, steps, SUB)),
        dma((4, 2)),
        dma(()),
        dma((groups,)),
        dma(()),
        dma((groups,)),
        dma((2,)),
        dma(()),
        dma((groups,)),
        dma((2, steps, SUB)),
        dma((2, steps, SUB)),
    ]
    anywhere = pl.BlockSpec(memory_space=pl.ANY)
    in_vmem = pl.BlockSpec(memory_space=pltpu.VMEM)
    return pl.pallas_call(
        functools.partial(kernel, grid3, slots),
        out_shape=(
            pltpu.VMEM((1, T, D), BF16),
            pltpu.VMEM((1, rows_z, FF), F32),
            pltpu.VMEM((1, rows_z, FF), F32),
            pltpu.VMEM((1, rows_z, FF), F32),
        ),
        in_specs=[anywhere] * 5
        + [in_vmem] * 4
        + [anywhere] * 3
        + [pl.BlockSpec(memory_space=pltpu.SMEM)],
        out_specs=(in_vmem,) * 4,
        scratch_shapes=scratch,
        compiler_params=pltpu.CompilerParams(
            collective_id=0, has_side_effects=True, vmem_limit_bytes=60 * 1024 * 1024
        ),
        name="layer",
    )(
        queries,
        keys,
        values,
        residual_in,
        cotangent,
        jnp.transpose(expert_ids, (0, 2, 1)),
        router.T,
        attn_gain.reshape(1, D),
        moe_gain.reshape(1, D),
        w_gate,
        w_up,
        w_down,
        trainable,
    )


def solution(mesh, grid3=(4, 4, 2)):
    blocks = P("dp", "seq", None)
    weights = P("seq", "dp", None)
    return jax.shard_map(
        functools.partial(body, grid3, mesh.shape["dp"]),
        mesh=mesh,
        in_specs=(blocks,) * 6 + (P(), P(), P()) + (weights,) * 3 + (P("seq"),),
        out_specs=(blocks, weights, weights, weights),
        check_vma=False,
    )
```

```python
import functools

import jax
import jax.numpy as jnp
from jax import lax
from jax.experimental import pallas as pl
from jax.experimental.pallas import tpu as pltpu
from jax.sharding import PartitionSpec as P

HD = 128
EPS = 1e-06
MESH = pl.DeviceIdType.MESH
F32 = jnp.float32
BF16 = jnp.bfloat16
Q = 4
GR = 4
SUB = 2


EARLY = ((), (), (), (0, 1, 2, 3, 4, 5, 6, 7))


def early(groups):
    return [[g for g in range(groups) if g * 8 // groups in at] for at in EARLY]


def dot(a, b, ca=1, cb=0):
    return lax.dot_general(a, b, (((ca,), (cb,)), ((), ())), preferred_element_type=F32)


def kernel(
    grid3,
    slots,
    q_in,
    k_in,
    v_in,
    res_in,
    cot_in,
    ids_ref,
    router_ref,
    again_ref,
    mgain_ref,
    wg_in,
    wu_in,
    wd_in,
    train_ref,
    mixed_ref,
    gg_ref,
    gu_ref,
    gd_ref,
    in_sem,
    q_ref,
    k_ref,
    v_ref,
    res_ref,
    cot_ref,
    w_all,
    st,
    sib,
    cs_send,
    cs_recv,
    pf_send,
    pf_recv,
    up_send,
    pfx,
    stream,
    nst,
    place,
    placeg,
    c_send,
    c_recv,
    x_send,
    x_recv,
    g_send,
    g_recv,
    xs,
    cs,
    pre,
    gcol,
    dgu,
    hid,
    hidg,
    r_send,
    r_recv,
    eo,
    gbuf,
    rs_send,
    rs_recv,
    ag_ss,
    ag_rs,
    p_sem,
    c_ss,
    c_rs,
    x_ss,
    x_rs,
    g_sem,
    r_ss,
    r_rs,
    rr_ss,
    rr_rs,
):
    ny, nx, nc = grid3
    ns = ny * nx * nc
    T, D = q_ref.shape
    H = D // HD
    DQ = D // Q
    FF = wg_in.shape[2]
    nz = w_all.shape[0]
    rows_z = w_all.shape[1]
    chips, PR = st.shape[1], st.shape[2]
    RB = Q * slots
    groups = ns // GR
    GB = GR * RB
    GX = GR * slots
    n_exp = router_ref.shape[0]

    mz = lax.axis_index("dp")
    ms = lax.axis_index("seq")
    mc = ms % nc
    mx = (ms // nc) % nx
    my = ms // (nc * nx)
    right, left = (mz + 1) % nz, (mz + nz - 1) % nz

    mchip = my * nx + mx

    def hops(p):
        dx, dy = (p // nc) % nx, p // (nc * nx)
        return min(dx, nx - dx) + min(dy, ny - dy)

    slot_list = [0] + sorted(range(1, ns), key=lambda p: -hops(p))

    def moved(p, sign):
        dc, dx, dy = p % nc, (p // nc) % nx, p // (nc * nx)
        c = (mc + sign * dc + nc) % nc
        x = (mx + sign * dx + nx) % nx
        y = (my + sign * dy + ny) % ny
        return (y * nx + x) * nc + c

    def shifted(k, sign):
        return moved(slot_list[k], sign)

    loads = {}
    for n, (name, src, dst) in enumerate(
        (
            ("k", k_in.at[0], k_ref),
            ("v", v_in.at[0], v_ref),
            ("gate", wg_in.at[0], w_all.at[mz, :, pl.ds(0, FF)]),
            ("up", wu_in.at[0], w_all.at[mz, :, pl.ds(FF, FF)]),
            ("down", wd_in.at[0], w_all.at[mz, :, pl.ds(2 * FF, FF)]),
            ("cot", cot_in.at[0], cot_ref),
            ("q", q_in.at[0], q_ref),
            ("res", res_in.at[0], res_ref),
        )
    ):
        loads[name] = pltpu.make_async_copy(src, dst, in_sem.at[n])
        loads[name].start()

    barrier = pltpu.get_barrier_semaphore()

    def greet(k, carry):
        pl.semaphore_signal(barrier, inc=1, device_id={"seq": moved(k, 1)}, device_id_type=MESH)
        return carry

    lax.fori_loop(1, ns, greet, 0)
    for z in (left, right):
        pl.semaphore_signal(barrier, inc=1, device_id={"dp": z}, device_id_type=MESH)

    for name in ("gate", "up", "down"):
        loads[name].wait()

    steps = nz // 2
    piece = rows_z // SUB
    near = (right, left)

    def order(way):
        return range(SUB) if way == 0 else range(SUB - 1, -1, -1)

    def far_half(way, u):
        return (u < SUB // 2) == (way == 0)

    def ag_copy(way, s, u):
        chunk = (mz + nz - s) % nz if way == 0 else (mz + s) % nz
        ref = w_all.at[chunk, pl.ds(u * piece, piece), :]
        return pltpu.make_async_remote_copy(
            src_ref=ref,
            dst_ref=ref,
            send_sem=ag_ss.at[way, s, u],
            recv_sem=ag_rs.at[way, s, u],
            device_id={"dp": near[way]},
            device_id_type=MESH,
        )

    def ag_wait(way, s, u):
        chunk = (mz + nz - 1 - s) % nz if way == 0 else (mz + 1 + s) % nz
        ref = w_all.at[chunk, pl.ds(u * piece, piece), :]
        pltpu.make_async_copy(ref, ref, ag_rs.at[way, s, u]).wait()

    def ag_used(way, s, u):
        return 0 <= s < steps and (s < steps - 1 or far_half(way, u))

    def pump(s, i):
        for way in (0, 1):
            u = order(way)[i]
            if ag_used(way, s - 1, u):
                ag_wait(way, s - 1, u)
            if ag_used(way, s, u):
                ag_copy(way, s, u).start()

    items = [(s, i) for s in range(steps + 1) for i in range(SUB)]

    def pump_to(s, i=SUB - 1):
        while items and items[0] <= (s, i):
            pump(*items.pop(0))

    loads["k"].wait()
    loads["v"].wait()
    n_piece = HD // PR
    for h in range(H):
        sl = slice(h * HD, (h + 1) * HD)
        state = dot(k_ref[:, sl], v_ref[:, sl], 0, 0).astype(BF16)
        for i in range(n_piece):
            p = h * n_piece + i
            st[p % nc, p // nc] = state[i * PR : (i + 1) * PR, :]

    eye = lax.broadcasted_iota(jnp.int32, (T, T), 0) == lax.broadcasted_iota(jnp.int32, (T, T), 1)
    ids = ids_ref[0].astype(F32)

    def as_col(row):
        return jnp.sum(jnp.where(eye, row, 0.0), axis=1, keepdims=True)

    id0, id1 = as_col(ids[0:1]).astype(jnp.int32), as_col(ids[1:2]).astype(jnp.int32)
    lane_e = lax.broadcasted_iota(jnp.int32, (T, n_exp), 1)
    hot0, hot1 = (lane_e == id0).astype(F32), (lane_e == id1).astype(F32)
    below = (
        lax.broadcasted_iota(jnp.int32, (T, T), 0) > lax.broadcasted_iota(jnp.int32, (T, T), 1)
    ).astype(F32)
    counts = dot(below.astype(BF16), (hot0 + hot1).astype(BF16))

    def as_row(col):
        return jnp.sum(jnp.where(eye, col, 0.0), axis=0, keepdims=True)

    def relative(ident):
        c, x, y = ident % nc, (ident // nc) % nx, ident // (nc * nx)
        return (((y - my + ny) % ny) * nx + (x - mx + nx) % nx) * nc + (c - mc + nc) % nc

    rank0 = jnp.sum(counts * hot0, axis=1, keepdims=True)
    rank1 = jnp.sum(counts * hot1, axis=1, keepdims=True)
    rel_n = relative(lax.broadcasted_iota(jnp.int32, (1, n_exp), 1))
    rel_e = jnp.zeros((1, n_exp), F32)
    for k in range(1, ns):
        rel_e = rel_e + jnp.where(rel_n == slot_list[k], float(k), 0.0)
    rel0 = jnp.sum(rel_e * hot0, axis=1, keepdims=True)
    rel1 = jnp.sum(rel_e * hot1, axis=1, keepdims=True)
    code0, code1 = rel0 * RB + rank0, rel1 * RB + rank1
    row0, row1 = as_row(code0).astype(jnp.int32), as_row(code1).astype(jnp.int32)
    icode0, icode1 = code0.astype(jnp.int32), code1.astype(jnp.int32)

    loads["cot"].wait()
    for q in range(Q):
        nst[q * T : (q + 1) * T, :] = cot_ref[:, q * DQ : (q + 1) * DQ]
    r_iota = lax.broadcasted_iota(jnp.int32, (GB, T), 0)
    for g in range(groups):
        for q in range(Q):
            at = r_iota + (g * GB - q * slots)
            hit = (at == row0) | (at == row1)
            place[g, :, q * T : (q + 1) * T] = jnp.where(hit, 1.0, 0.0).astype(BF16)

    half_g = max(1, groups // 2)

    def fill(part, buf):
        rows = place[pl.ds(part * half_g, half_g)].reshape(half_g * GB, Q * T)
        got = dot(rows, nst[...]).astype(BF16)
        buf[pl.ds(part * half_g * GR, half_g * GR)] = got.reshape(half_g * GR, RB, DQ)

    def send_slot(k, src, dst, ss, rs, sign):
        return pltpu.make_async_remote_copy(
            src_ref=src.at[k],
            dst_ref=dst.at[k],
            send_sem=ss,
            recv_sem=rs,
            device_id={"seq": shifted(k, sign)},
            device_id_type=MESH,
        )

    def send_group(g, src, dst, ss, rs, sign):
        for i in range(GR):
            if g * GR + i > 0:
                send_slot(g * GR + i, src, dst, ss, rs.at[g], sign).start()

    def group_ref(g, buf):
        first = 1 if g == 0 else 0
        return buf.at[pl.ds(g * GR + first, GR - first)]

    for part in range(groups // half_g):
        fill(part, c_send)

    g_rows = lax.broadcasted_iota(jnp.int32, (ns * 16, T), 0)
    grow0 = as_row(rel0 * 16 + rank0).astype(jnp.int32)
    grow1 = as_row(rel1 * 16 + rank1).astype(jnp.int32)

    def wide(col):
        return jnp.broadcast_to(col.astype(F32), (T, 128)).astype(BF16)

    g_msg = dot(jnp.where(g_rows == grow0, 1.0, 0.0).astype(BF16), wide(id1)) + dot(
        jnp.where(g_rows == grow1, 1.0, 0.0).astype(BF16), wide(id0)
    )
    g_send[...] = g_msg.astype(BF16).reshape(ns, 16, 128)

    loads["q"].wait()
    causal = lax.broadcasted_iota(jnp.int32, (T, T), 0) >= lax.broadcasted_iota(
        jnp.int32, (T, T), 1
    )
    for h in range(H):
        sl = slice(h * HD, (h + 1) * HD)
        scores = dot(q_ref[:, sl], k_ref[:, sl], 1, 1)
        weights = jnp.where(causal, scores, 0.0).astype(BF16)
        stream[:, sl] = dot(weights, v_ref[:, sl])
    loads["res"].wait()

    pl.semaphore_wait(barrier, ns - 1 + 2)
    pump_to(0)

    sibling = mchip * nc + (1 - mc)
    pair_a = pltpu.make_async_remote_copy(
        src_ref=st.at[1 - mc],
        dst_ref=sib,
        send_sem=p_sem.at[0, 0],
        recv_sem=p_sem.at[0, 1],
        device_id={"seq": sibling},
        device_id_type=MESH,
    )
    pair_a.start()
    for g in early(groups)[0]:
        send_group(g, c_send, c_recv, c_ss, c_rs, 1)
    for k in range(1, ns):
        send_slot(k, g_send, g_recv, g_sem.at[0], g_sem.at[1], 1).start()
    g_recv[0] = g_send[0]

    def wait_bytes(ref, sem):
        pltpu.make_async_copy(ref, ref, sem).wait()

    def send_pieces(src, dst, which):
        for p in sorted(range(1, chips), key=lambda p: -hops(p * nc)):
            to = moved(p * nc, 1)
            pltpu.make_async_remote_copy(
                src_ref=src.at[to // nc],
                dst_ref=dst.at[mchip],
                send_sem=p_sem.at[which, 0],
                recv_sem=p_sem.at[which, 1],
                device_id={"seq": to},
                device_id_type=MESH,
            ).start()

    pair_a.wait_recv()
    cs_send[...] = (st[mc].astype(F32) + sib[...].astype(F32)).astype(BF16)

    send_pieces(cs_send, cs_recv, 1)
    cs_recv[mchip] = cs_send[mchip]
    pump_to(1, 0)
    for g in early(groups)[1]:
        send_group(g, c_send, c_recv, c_ss, c_rs, 1)

    pump_to(1)
    wait_bytes(cs_recv.at[pl.ds(0, chips - 1)], p_sem.at[1, 1])
    acc = jnp.zeros((PR, HD), F32)
    for j in range(chips):
        pf_send[j] = acc.astype(BF16)
        acc = acc + cs_recv[j].astype(F32)
    send_pieces(pf_send, pf_recv, 2)
    pf_recv[mchip] = pf_send[mchip]
    pump_to(2, 0)
    for g in early(groups)[2]:
        send_group(g, c_send, c_recv, c_ss, c_rs, 1)
    pump_to(2)

    second = mc.astype(F32)
    wait_bytes(pf_recv.at[pl.ds(0, chips - 1)], p_sem.at[2, 1])
    got = pf_recv[...].astype(F32)
    up_send[...] = (got + (1.0 - second) * st[mc].astype(F32)).astype(BF16)
    pair_b = pltpu.make_async_remote_copy(
        src_ref=up_send,
        dst_ref=pfx.at[mc],
        send_sem=p_sem.at[3, 0],
        recv_sem=p_sem.at[3, 1],
        device_id={"seq": sibling},
        device_id_type=MESH,
    )
    pair_b.start()
    pfx[mc] = (got + second * sib[...].astype(F32)).astype(BF16)
    for g in early(groups)[3]:
        send_group(g, c_send, c_recv, c_ss, c_rs, 1)
    c_recv[0] = c_send[0]
    pump_to(3, 0)
    pair_b.wait_recv()

    squares = jnp.zeros((T, HD), F32)
    for h in range(H):
        sl = slice(h * HD, (h + 1) * HD)
        ps = range(h * n_piece, (h + 1) * n_piece)
        prefix = jnp.concatenate([pfx[p % nc, p // nc] for p in ps], axis=0)
        att = stream[:, sl] + dot(q_ref[:, sl], prefix)
        att = att * lax.rsqrt(jnp.mean(att * att, axis=-1, keepdims=True) + EPS)
        one = res_ref[:, sl].astype(F32) + att * again_ref[:, sl]
        stream[:, sl] = one
        squares = squares + one * one
        if h == H // 2:
            pump_to(3)
    scale = lax.rsqrt(jnp.sum(squares, axis=-1, keepdims=True) / D + EPS)
    logits = jnp.zeros((T, n_exp), F32)
    for q in range(Q):
        cols = slice(q * DQ, (q + 1) * DQ)
        part = (stream[:, cols] * scale * mgain_ref[:, cols]).astype(BF16)
        nst[q * T : (q + 1) * T, :] = part
        logits = logits + dot(part, router_ref[:, cols], 1, 1)
    pump_to(4, 0)

    for part in range(groups // half_g):
        fill(part, x_send)
        for g in range(part * half_g, (part + 1) * half_g):
            send_group(g, x_send, x_recv, x_ss, x_rs, 1)
    pump_to(4)
    x_recv[0] = x_send[0]

    sig0 = jax.nn.sigmoid(jnp.sum(hot0 * logits, axis=1, keepdims=True))
    sig1 = jax.nn.sigmoid(jnp.sum(hot1 * logits, axis=1, keepdims=True))
    gate0, gate1 = sig0 / (sig0 + sig1), sig1 / (sig0 + sig1)
    pump_to(5, 0)

    l_iota = lax.broadcasted_iota(jnp.int32, (T, GB), 1)
    for g in range(groups):
        for q in range(Q):
            at = l_iota + (g * GB - q * slots)
            val = jnp.where(at == icode0, gate0, 0.0) + jnp.where(at == icode1, gate1, 0.0)
            placeg[q * T : (q + 1) * T, g * GB : (g + 1) * GB] = val.astype(BF16)
    pump_to(5)

    o = lax.broadcasted_iota(jnp.int32, (GB, GB), 0)
    c = lax.broadcasted_iota(jnp.int32, (GB, GB), 1)
    want = ((o // slots) % GR) * RB + (o // GX) * slots + o % slots
    perm = (c == want).astype(F32).astype(BF16)

    def unpack(g, src, dst):
        got = dot(perm, src[pl.ds(g * GR, GR)].reshape(GB, DQ)).astype(BF16)
        for q in range(Q):
            dst[g * GX : (g + 1) * GX, q * DQ : (q + 1) * DQ] = got[q * GX : (q + 1) * GX, :]

    KB = rows_z * 2

    def matmul_rows(src, rows, c0, c1):
        def one(i, carry):
            cols = pl.ds(pl.multiple_of(i * KB, KB), KB)
            w = w_all[pl.ds(2 * i, 2), :, c0:c1].reshape(KB, c1 - c0)
            pre[rows, c0:c1] += dot(src[rows, cols], w)
            return carry

        lax.fori_loop(0, nz // 2, one, 0)

    pump_to(steps)
    pre[...] = jnp.zeros_like(pre)
    wait_bytes(g_recv.at[pl.ds(1, ns - 1)], g_sem.at[1])
    o16 = lax.broadcasted_iota(jnp.int32, (GX, GR * 16), 0)
    c16 = lax.broadcasted_iota(jnp.int32, (GX, GR * 16), 1)
    pick = (c16 == (o16 // slots) * 16 + o16 % slots).astype(F32).astype(BF16)
    for g in range(groups):
        got = dot(pick, g_recv[pl.ds(g * GR, GR)].reshape(GR * 16, 128))
        gcol[g * GX : (g + 1) * GX, :] = got[:, 0:1]
    for g in range(groups):
        wait_bytes(group_ref(g, c_recv), c_rs.at[g])
        unpack(g, c_recv, cs)
    R = ns * slots
    matmul_rows(cs, slice(0, R), 2 * FF, 3 * FF)
    first_half = groups // 2
    for g in range(first_half):
        wait_bytes(group_ref(g, x_recv), x_rs.at[g])
        unpack(g, x_recv, xs)
    cut = first_half * GX

    def row_gates(a, b):
        lane_r = lax.broadcasted_iota(jnp.int32, (b - a, n_exp), 1)
        row_logits = dot(xs[a:b, :], router_ref[...], 1, 1)
        own = jnp.sum(jnp.where(lane_r == ms, row_logits, 0.0), axis=1, keepdims=True)
        hit = lane_r.astype(F32) == gcol[a:b, :]
        other = jnp.sum(jnp.where(hit, row_logits, 0.0), axis=1, keepdims=True)
        own, other = jax.nn.sigmoid(own), jax.nn.sigmoid(other)
        gcol[a:b, :] = own / (own + other)

    if cut:
        matmul_rows(xs, slice(0, cut), 0, 2 * FF)
        row_gates(0, cut)
    for g in range(first_half, groups):
        wait_bytes(group_ref(g, x_recv), x_rs.at[g])
        unpack(g, x_recv, xs)
    matmul_rows(xs, slice(cut, R), 0, 2 * FF)
    row_gates(cut, R)
    gates = gcol[...]
    pre_gate = pre[:, 0:FF]
    pre_up = pre[:, FF : 2 * FF]
    d_hidden = pre[:, 2 * FF : 3 * FF] * gates
    sigma = jax.nn.sigmoid(pre_gate)
    act = pre_gate * sigma
    hidden = (act * pre_up).astype(BF16)
    hid[...] = hidden
    hidg[...] = (hidden.astype(F32) * gates).astype(BF16)
    dgu[:, 0:FF] = (d_hidden * pre_up * sigma * (1.0 + pre_gate * (1.0 - sigma))).astype(BF16)
    dgu[:, FF : 2 * FF] = (d_hidden * act).astype(BF16)

    half = rows_z // SUB

    def grad_of(chunk):
        cols = pl.ds(pl.multiple_of(chunk * rows_z, rows_z), rows_z)
        return dot(xs[:, cols], dgu[...], 0, 0), dot(cs[:, cols], hidg[...], 0, 0)

    def rs_copy(way, s, u):
        return pltpu.make_async_remote_copy(
            src_ref=rs_send.at[way, s, pl.ds(u * half, half)],
            dst_ref=rs_recv.at[way, s, pl.ds(u * half, half)],
            send_sem=rr_ss.at[way, s, u],
            recv_sem=rr_rs.at[way, s, u],
            device_id={"dp": near[way]},
            device_id_type=MESH,
        )

    def rs_used(way, s, u):
        return 0 <= s < steps and (s > 0 or far_half(way, u))

    def rs_order(way):
        return range(SUB - 1, -1, -1) if way == 0 else range(SUB)

    def rs_grads(s):
        at = [
            pl.ds(pl.multiple_of(chunk * rows_z, rows_z), rows_z)
            for chunk in ((mz + steps - s) % nz, (mz + nz - steps + s) % nz)
        ]
        if s == 0:
            at = at[:1]
        a = dot(jnp.concatenate([xs[:, c] for c in at], axis=1), dgu[...], 0, 0)
        b = dot(jnp.concatenate([cs[:, c] for c in at], axis=1), hidg[...], 0, 0)
        for way in range(len(at)):
            gbuf[way, :, 0 : 2 * FF] = a[way * rows_z : (way + 1) * rows_z]
            gbuf[way, :, 2 * FF : 3 * FF] = b[way * rows_z : (way + 1) * rows_z]

    def rs_piece(way, s, u):
        rows = slice(u * half, (u + 1) * half)
        val = gbuf[0 if s == 0 else way, rows, :]
        if rs_used(way, s - 1, u):
            rs_copy(way, s - 1, u).wait_recv()
            val = val + rs_recv[way, s - 1, rows, :].astype(F32)
        rs_send[way, s, rows, :] = val.astype(BF16)
        rs_copy(way, s, u).start()

    def rs_pieces(s, when):
        for i in range(SUB):
            for way in (0, 1):
                u = rs_order(way)[i]
                if rs_used(way, s, u) and when(rs_used(way, s - 1, u)):
                    rs_piece(way, s, u)

    def always(waits):
        return True

    rs_grads(0)
    rs_pieces(0, always)
    rs_grads(1)
    rs_pieces(1, lambda waits: not waits)

    for q in range(Q):
        n = nz // Q
        w_q = w_all[q * n : (q + 1) * n, :, 2 * FF : 3 * FF].reshape(DQ, FF)
        got = dot(hid[...], w_q, 1, 1).astype(BF16)
        for g in range(groups):
            eo[g, q * GX : (q + 1) * GX, :] = got[g * GX : (g + 1) * GX, :]
    for g in range(groups):
        r_send[pl.ds(g * GR, GR)] = dot(perm, eo[g], 0, 0).astype(BF16).reshape(GR, RB, DQ)
        send_group(g, r_send, r_recv, r_ss, r_rs, -1)
    r_recv[0] = r_send[0]

    rs_pieces(1, lambda waits: waits)
    first_mix = min(5, steps)

    for s in range(2, steps + 1):
        if s < steps:
            rs_grads(s)
            rs_pieces(s, always)
        if s == first_mix:
            for g in range(groups):
                wait_bytes(group_ref(g, r_recv), r_rs.at[g])
        for q in range(Q):
            if s == min(first_mix + q, steps):
                cols = slice(q * DQ, (q + 1) * DQ)
                back = r_recv[...].reshape(ns * RB, DQ)
                got = dot(placeg[q * T : (q + 1) * T, :], back)
                mixed_ref[0, :, cols] = (stream[:, cols] + got).astype(BF16)

    a, b = grad_of(mz)
    gbuf[0, :, 0 : 2 * FF] = a
    gbuf[0, :, 2 * FF : 3 * FF] = b
    flag = (train_ref[0] > 0).astype(F32)
    for way in (0, 1):
        for u in rs_order(way):
            rows = slice(u * half, (u + 1) * half)
            rs_copy(way, steps - 1, u).wait_recv()
            gbuf[0, rows, :] = gbuf[0, rows, :] + rs_recv[way, steps - 1, rows, :].astype(F32)
    gg_ref[0] = gbuf[0, :, 0:FF] * flag
    gu_ref[0] = gbuf[0, :, FF : 2 * FF] * flag
    gd_ref[0] = gbuf[0, :, 2 * FF : 3 * FF] * flag

    for way in (0, 1):
        for s in range(steps):
            for u in range(SUB):
                if ag_used(way, s, u):
                    ag_copy(way, s, u).wait_send()
                if rs_used(way, s, u):
                    rs_copy(way, s, u).wait_send()
    pair_a.wait_send()
    pair_b.wait_send()
    wait_bytes(cs_send.at[pl.ds(0, chips - 1)], p_sem.at[1, 0])
    wait_bytes(pf_send.at[pl.ds(0, chips - 1)], p_sem.at[2, 0])
    wait_bytes(c_send.at[pl.ds(1, ns - 1)], c_ss)
    wait_bytes(x_send.at[pl.ds(1, ns - 1)], x_ss)
    wait_bytes(g_send.at[pl.ds(1, ns - 1)], g_sem.at[0])
    wait_bytes(r_send.at[pl.ds(1, ns - 1)], r_ss)


def leave(*refs):
    n = len(refs) // 2
    sems = refs[-1]
    copies = [pltpu.make_async_copy(refs[i], refs[n + i], sems.at[i]) for i in range(n)]
    for c in copies:
        c.start()
    for c in copies:
        c.wait()


def body(
    grid3,
    nz,
    queries,
    keys,
    values,
    residual_in,
    cotangent,
    expert_ids,
    router,
    attn_gain,
    moe_gain,
    w_gate,
    w_up,
    w_down,
    trainable,
):
    ns = grid3[0] * grid3[1] * grid3[2]
    T, D = queries.shape[1:]
    H = D // HD
    FF = w_gate.shape[2]
    slots = max(2, 3 * T // ns)
    rows_z = w_gate.shape[1]
    RB, DQ, R = Q * slots, D // Q, ns * slots
    PR = H * HD // ns
    groups = ns // GR
    steps = nz // 2
    nc = grid3[2]
    chips = ns // nc
    vm = pltpu.VMEM
    dma = pltpu.SemaphoreType.DMA
    scratch = [
        dma((8,)),
        vm((T, D), BF16),
        vm((T, D), BF16),
        vm((T, D), BF16),
        vm((T, D), BF16),
        vm((T, D), BF16),
        vm((nz, rows_z, 3 * FF), BF16),
        vm((nc, chips, PR, HD), BF16),
        vm((chips, PR, HD), BF16),
        vm((chips, PR, HD), BF16),
        vm((chips, PR, HD), BF16),
        vm((chips, PR, HD), BF16),
        vm((chips, PR, HD), BF16),
        vm((chips, PR, HD), BF16),
        vm((nc, chips, PR, HD), BF16),
        vm((T, D), F32),
        vm((Q * T, DQ), BF16),
        vm((groups, GR * RB, Q * T), BF16),
        vm((Q * T, ns * RB), BF16),
        vm((ns, RB, DQ), BF16),
        vm((ns, RB, DQ), BF16),
        vm((ns, RB, DQ), BF16),
        vm((ns, RB, DQ), BF16),
        vm((ns, 16, 128), BF16),
        vm((ns, 16, 128), BF16),
        vm((R, D), BF16),
        vm((R, D), BF16),
        vm((R, 3 * FF), F32),
        vm((R, 1), F32),
        vm((R, 2 * FF), BF16),
        vm((R, FF), BF16),
        vm((R, FF), BF16),
        vm((ns, RB, DQ), BF16),
        vm((ns, RB, DQ), BF16),
        vm((groups, GR * RB, DQ), BF16),
        vm((2, rows_z, 3 * FF), F32),
        vm((2, steps, rows_z, 3 * FF), BF16),
        vm((2, steps, rows_z, 3 * FF), BF16),
        dma((2, steps, SUB)),
        dma((2, steps, SUB)),
        dma((4, 2)),
        dma(()),
        dma((groups,)),
        dma(()),
        dma((groups,)),
        dma((2,)),
        dma(()),
        dma((groups,)),
        dma((2, steps, SUB)),
        dma((2, steps, SUB)),
    ]
    anywhere = pl.BlockSpec(memory_space=pl.ANY)
    in_vmem = pl.BlockSpec(memory_space=pltpu.VMEM)
    outs = pl.pallas_call(
        functools.partial(kernel, grid3, slots),
        out_shape=(
            pltpu.VMEM((1, T, D), BF16),
            pltpu.VMEM((1, rows_z, FF), F32),
            pltpu.VMEM((1, rows_z, FF), F32),
            pltpu.VMEM((1, rows_z, FF), F32),
        ),
        in_specs=[anywhere] * 5
        + [in_vmem] * 4
        + [anywhere] * 3
        + [pl.BlockSpec(memory_space=pltpu.SMEM)],
        out_specs=(in_vmem,) * 4,
        scratch_shapes=scratch,
        compiler_params=pltpu.CompilerParams(
            collective_id=0, has_side_effects=True, vmem_limit_bytes=60 * 1024 * 1024
        ),
        name="layer",
    )(
        queries,
        keys,
        values,
        residual_in,
        cotangent,
        jnp.transpose(expert_ids, (0, 2, 1)),
        router.T,
        attn_gain.reshape(1, D),
        moe_gain.reshape(1, D),
        w_gate,
        w_up,
        w_down,
        trainable,
    )
    return pl.pallas_call(
        leave,
        out_shape=tuple(jax.ShapeDtypeStruct(o.shape, o.dtype) for o in outs),
        in_specs=[in_vmem] * len(outs),
        out_specs=(anywhere,) * len(outs),
        scratch_shapes=[dma((len(outs),))],
        name="leave",
    )(*(pltpu.with_memory_space_constraint(o, pltpu.VMEM) for o in outs))


def solution(mesh, grid3=(4, 4, 2)):
    blocks = P("dp", "seq", None)
    weights = P("seq", "dp", None)
    return jax.shard_map(
        functools.partial(body, grid3, mesh.shape["dp"]),
        mesh=mesh,
        in_specs=(blocks,) * 6 + (P(), P(), P()) + (weights,) * 3 + (P("seq"),),
        out_specs=(blocks, weights, weights, weights),
        check_vma=False,
    )
```

```python
import functools

import jax
import jax.numpy as jnp
from jax import lax
from jax.experimental import pallas as pl
from jax.experimental.pallas import tpu as pltpu
from jax.sharding import PartitionSpec as P

HD = 128
EPS = 1e-06
MESH = pl.DeviceIdType.MESH
F32 = jnp.float32
BF16 = jnp.bfloat16
Q = 4
GR = 4
SUB = 2


EARLY = ((), (), (), (0, 1, 2, 3, 4, 5, 6, 7))


def early(groups):
    return [[g for g in range(groups) if g * 8 // groups in at] for at in EARLY]


def dot(a, b, ca=1, cb=0):
    return lax.dot_general(a, b, (((ca,), (cb,)), ((), ())), preferred_element_type=F32)


def kernel(
    grid3,
    slots,
    q_in,
    k_in,
    v_in,
    res_in,
    cot_in,
    ids_ref,
    router_ref,
    again_ref,
    mgain_ref,
    wg_in,
    wu_in,
    wd_in,
    train_ref,
    mixed_ref,
    gg_ref,
    gu_ref,
    gd_ref,
    in_sem,
    q_ref,
    k_ref,
    v_ref,
    res_ref,
    cot_ref,
    w_all,
    st,
    sib,
    cs_send,
    cs_recv,
    pf_send,
    pf_recv,
    up_send,
    pfx,
    stream,
    nst,
    place,
    placeg,
    c_send,
    c_recv,
    x_send,
    x_recv,
    g_send,
    g_recv,
    xs,
    cs,
    pre,
    gcol,
    dgu,
    hid,
    hidg,
    r_send,
    r_recv,
    eo,
    gbuf,
    rs_send,
    rs_recv,
    ag_ss,
    ag_rs,
    p_sem,
    c_ss,
    c_rs,
    x_ss,
    x_rs,
    g_sem,
    r_ss,
    r_rs,
    rr_ss,
    rr_rs,
):
    ny, nx, nc = grid3
    ns = ny * nx * nc
    T, D = q_ref.shape
    H = D // HD
    DQ = D // Q
    FF = wg_in.shape[2]
    nz = w_all.shape[0]
    rows_z = w_all.shape[1]
    chips, PR = st.shape[1], st.shape[2]
    RB = Q * slots
    groups = ns // GR
    GB = GR * RB
    GX = GR * slots
    n_exp = router_ref.shape[0]

    mz = lax.axis_index("dp")
    ms = lax.axis_index("seq")
    mc = ms % nc
    mx = (ms // nc) % nx
    my = ms // (nc * nx)
    right, left = (mz + 1) % nz, (mz + nz - 1) % nz

    mchip = my * nx + mx

    def hops(p):
        dx, dy = (p // nc) % nx, p // (nc * nx)
        return min(dx, nx - dx) + min(dy, ny - dy)

    slot_list = [0] + sorted(range(1, ns), key=lambda p: -hops(p))

    def moved(p, sign):
        dc, dx, dy = p % nc, (p // nc) % nx, p // (nc * nx)
        c = (mc + sign * dc + nc) % nc
        x = (mx + sign * dx + nx) % nx
        y = (my + sign * dy + ny) % ny
        return (y * nx + x) * nc + c

    def shifted(k, sign):
        return moved(slot_list[k], sign)

    loads = {}
    for n, (name, src, dst) in enumerate(
        (
            ("k", k_in.at[0], k_ref),
            ("v", v_in.at[0], v_ref),
            ("gate", wg_in.at[0], w_all.at[mz, :, pl.ds(0, FF)]),
            ("up", wu_in.at[0], w_all.at[mz, :, pl.ds(FF, FF)]),
            ("down", wd_in.at[0], w_all.at[mz, :, pl.ds(2 * FF, FF)]),
            ("cot", cot_in.at[0], cot_ref),
            ("q", q_in.at[0], q_ref),
            ("res", res_in.at[0], res_ref),
        )
    ):
        loads[name] = pltpu.make_async_copy(src, dst, in_sem.at[n])
        loads[name].start()

    barrier = pltpu.get_barrier_semaphore()

    def greet(k, carry):
        pl.semaphore_signal(barrier, inc=1, device_id={"seq": moved(k, 1)}, device_id_type=MESH)
        return carry

    lax.fori_loop(1, ns, greet, 0)
    for z in (left, right):
        pl.semaphore_signal(barrier, inc=1, device_id={"dp": z}, device_id_type=MESH)

    for name in ("gate", "up", "down"):
        loads[name].wait()

    steps = nz // 2
    piece = rows_z // SUB
    near = (right, left)

    def order(way):
        return range(SUB) if way == 0 else range(SUB - 1, -1, -1)

    def far_half(way, u):
        return (u < SUB // 2) == (way == 0)

    def ag_copy(way, s, u):
        chunk = (mz + nz - s) % nz if way == 0 else (mz + s) % nz
        ref = w_all.at[chunk, pl.ds(u * piece, piece), :]
        return pltpu.make_async_remote_copy(
            src_ref=ref,
            dst_ref=ref,
            send_sem=ag_ss.at[way, s, u],
            recv_sem=ag_rs.at[way, s, u],
            device_id={"dp": near[way]},
            device_id_type=MESH,
        )

    def ag_wait(way, s, u):
        chunk = (mz + nz - 1 - s) % nz if way == 0 else (mz + 1 + s) % nz
        ref = w_all.at[chunk, pl.ds(u * piece, piece), :]
        pltpu.make_async_copy(ref, ref, ag_rs.at[way, s, u]).wait()

    def ag_used(way, s, u):
        return 0 <= s < steps and (s < steps - 1 or far_half(way, u))

    def pump(s, i):
        for way in (0, 1):
            u = order(way)[i]
            if ag_used(way, s - 1, u):
                ag_wait(way, s - 1, u)
            if ag_used(way, s, u):
                ag_copy(way, s, u).start()

    items = [(s, i) for s in range(steps + 1) for i in range(SUB)]

    def pump_to(s, i=SUB - 1):
        while items and items[0] <= (s, i):
            pump(*items.pop(0))

    loads["k"].wait()
    loads["v"].wait()
    n_piece = HD // PR
    for h in range(H):
        sl = slice(h * HD, (h + 1) * HD)
        state = dot(k_ref[:, sl], v_ref[:, sl], 0, 0).astype(BF16)
        for i in range(n_piece):
            p = h * n_piece + i
            st[p % nc, p // nc] = state[i * PR : (i + 1) * PR, :]

    eye = lax.broadcasted_iota(jnp.int32, (T, T), 0) == lax.broadcasted_iota(jnp.int32, (T, T), 1)
    ids = ids_ref[0].astype(F32)

    def as_col(row):
        return jnp.sum(jnp.where(eye, row, 0.0), axis=1, keepdims=True)

    id0, id1 = as_col(ids[0:1]).astype(jnp.int32), as_col(ids[1:2]).astype(jnp.int32)
    lane_e = lax.broadcasted_iota(jnp.int32, (T, n_exp), 1)
    hot0, hot1 = (lane_e == id0).astype(F32), (lane_e == id1).astype(F32)
    below = (
        lax.broadcasted_iota(jnp.int32, (T, T), 0) > lax.broadcasted_iota(jnp.int32, (T, T), 1)
    ).astype(F32)
    counts = dot(below.astype(BF16), (hot0 + hot1).astype(BF16))

    def as_row(col):
        return jnp.sum(jnp.where(eye, col, 0.0), axis=0, keepdims=True)

    def relative(ident):
        c, x, y = ident % nc, (ident // nc) % nx, ident // (nc * nx)
        return (((y - my + ny) % ny) * nx + (x - mx + nx) % nx) * nc + (c - mc + nc) % nc

    rank0 = jnp.sum(counts * hot0, axis=1, keepdims=True)
    rank1 = jnp.sum(counts * hot1, axis=1, keepdims=True)
    rel_n = relative(lax.broadcasted_iota(jnp.int32, (1, n_exp), 1))
    rel_e = jnp.zeros((1, n_exp), F32)
    for k in range(1, ns):
        rel_e = rel_e + jnp.where(rel_n == slot_list[k], float(k), 0.0)
    rel0 = jnp.sum(rel_e * hot0, axis=1, keepdims=True)
    rel1 = jnp.sum(rel_e * hot1, axis=1, keepdims=True)
    code0, code1 = rel0 * RB + rank0, rel1 * RB + rank1
    row0, row1 = as_row(code0).astype(jnp.int32), as_row(code1).astype(jnp.int32)
    icode0, icode1 = code0.astype(jnp.int32), code1.astype(jnp.int32)

    loads["cot"].wait()
    for q in range(Q):
        nst[q * T : (q + 1) * T, :] = cot_ref[:, q * DQ : (q + 1) * DQ]
    r_iota = lax.broadcasted_iota(jnp.int32, (GB, T), 0)
    for g in range(groups):
        for q in range(Q):
            at = r_iota + (g * GB - q * slots)
            hit = (at == row0) | (at == row1)
            place[g, :, q * T : (q + 1) * T] = jnp.where(hit, 1.0, 0.0).astype(BF16)

    half_g = max(1, groups // 2)

    def fill(part, buf):
        rows = place[pl.ds(part * half_g, half_g)].reshape(half_g * GB, Q * T)
        got = dot(rows, nst[...]).astype(BF16)
        buf[pl.ds(part * half_g * GR, half_g * GR)] = got.reshape(half_g * GR, RB, DQ)

    def send_slot(k, src, dst, ss, rs, sign):
        return pltpu.make_async_remote_copy(
            src_ref=src.at[k],
            dst_ref=dst.at[k],
            send_sem=ss,
            recv_sem=rs,
            device_id={"seq": shifted(k, sign)},
            device_id_type=MESH,
        )

    def send_group(g, src, dst, ss, rs, sign):
        for i in range(GR):
            if g * GR + i > 0:
                send_slot(g * GR + i, src, dst, ss, rs.at[g], sign).start()

    def group_ref(g, buf):
        first = 1 if g == 0 else 0
        return buf.at[pl.ds(g * GR + first, GR - first)]

    for part in range(groups // half_g):
        fill(part, c_send)

    g_rows = lax.broadcasted_iota(jnp.int32, (ns * 16, T), 0)
    grow0 = as_row(rel0 * 16 + rank0).astype(jnp.int32)
    grow1 = as_row(rel1 * 16 + rank1).astype(jnp.int32)

    def wide(col):
        return jnp.broadcast_to(col.astype(F32), (T, 128)).astype(BF16)

    g_msg = dot(jnp.where(g_rows == grow0, 1.0, 0.0).astype(BF16), wide(id1)) + dot(
        jnp.where(g_rows == grow1, 1.0, 0.0).astype(BF16), wide(id0)
    )
    g_send[...] = g_msg.astype(BF16).reshape(ns, 16, 128)

    pl.semaphore_wait(barrier, ns - 1 + 2)
    pump_to(0)

    sibling = mchip * nc + (1 - mc)
    pair_a = pltpu.make_async_remote_copy(
        src_ref=st.at[1 - mc],
        dst_ref=sib,
        send_sem=p_sem.at[0, 0],
        recv_sem=p_sem.at[0, 1],
        device_id={"seq": sibling},
        device_id_type=MESH,
    )
    pair_a.start()
    for g in early(groups)[0]:
        send_group(g, c_send, c_recv, c_ss, c_rs, 1)
    for k in range(1, ns):
        send_slot(k, g_send, g_recv, g_sem.at[0], g_sem.at[1], 1).start()
    g_recv[0] = g_send[0]

    def wait_bytes(ref, sem):
        pltpu.make_async_copy(ref, ref, sem).wait()

    def send_pieces(src, dst, which):
        for p in sorted(range(1, chips), key=lambda p: -hops(p * nc)):
            to = moved(p * nc, 1)
            pltpu.make_async_remote_copy(
                src_ref=src.at[to // nc],
                dst_ref=dst.at[mchip],
                send_sem=p_sem.at[which, 0],
                recv_sem=p_sem.at[which, 1],
                device_id={"seq": to},
                device_id_type=MESH,
            ).start()

    loads["q"].wait()
    causal = lax.broadcasted_iota(jnp.int32, (T, T), 0) >= lax.broadcasted_iota(
        jnp.int32, (T, T), 1
    )
    for h in range(H):
        sl = slice(h * HD, (h + 1) * HD)
        scores = dot(q_ref[:, sl], k_ref[:, sl], 1, 1)
        weights = jnp.where(causal, scores, 0.0).astype(BF16)
        stream[:, sl] = dot(weights, v_ref[:, sl])
    loads["res"].wait()

    pair_a.wait_recv()
    cs_send[...] = (st[mc].astype(F32) + sib[...].astype(F32)).astype(BF16)

    send_pieces(cs_send, cs_recv, 1)
    cs_recv[mchip] = cs_send[mchip]
    pump_to(1, 0)
    for g in early(groups)[1]:
        send_group(g, c_send, c_recv, c_ss, c_rs, 1)

    pump_to(1)
    wait_bytes(cs_recv.at[pl.ds(0, chips - 1)], p_sem.at[1, 1])
    acc = jnp.zeros((PR, HD), F32)
    for j in range(chips):
        pf_send[j] = acc.astype(BF16)
        acc = acc + cs_recv[j].astype(F32)
    send_pieces(pf_send, pf_recv, 2)
    pf_recv[mchip] = pf_send[mchip]
    pump_to(2, 0)
    for g in early(groups)[2]:
        send_group(g, c_send, c_recv, c_ss, c_rs, 1)
    pump_to(2)

    second = mc.astype(F32)
    wait_bytes(pf_recv.at[pl.ds(0, chips - 1)], p_sem.at[2, 1])
    got = pf_recv[...].astype(F32)
    up_send[...] = (got + (1.0 - second) * st[mc].astype(F32)).astype(BF16)
    pair_b = pltpu.make_async_remote_copy(
        src_ref=up_send,
        dst_ref=pfx.at[mc],
        send_sem=p_sem.at[3, 0],
        recv_sem=p_sem.at[3, 1],
        device_id={"seq": sibling},
        device_id_type=MESH,
    )
    pair_b.start()
    pfx[mc] = (got + second * sib[...].astype(F32)).astype(BF16)
    for g in early(groups)[3]:
        send_group(g, c_send, c_recv, c_ss, c_rs, 1)
    c_recv[0] = c_send[0]
    pump_to(3, 0)
    pair_b.wait_recv()

    squares = jnp.zeros((T, HD), F32)
    for h in range(H):
        sl = slice(h * HD, (h + 1) * HD)
        ps = range(h * n_piece, (h + 1) * n_piece)
        prefix = jnp.concatenate([pfx[p % nc, p // nc] for p in ps], axis=0)
        att = stream[:, sl] + dot(q_ref[:, sl], prefix)
        att = att * lax.rsqrt(jnp.mean(att * att, axis=-1, keepdims=True) + EPS)
        one = res_ref[:, sl].astype(F32) + att * again_ref[:, sl]
        stream[:, sl] = one
        squares = squares + one * one
        if h == H // 2:
            pump_to(3)
    scale = lax.rsqrt(jnp.sum(squares, axis=-1, keepdims=True) / D + EPS)
    logits = jnp.zeros((T, n_exp), F32)
    for q in range(Q):
        cols = slice(q * DQ, (q + 1) * DQ)
        part = (stream[:, cols] * scale * mgain_ref[:, cols]).astype(BF16)
        nst[q * T : (q + 1) * T, :] = part
        logits = logits + dot(part, router_ref[:, cols], 1, 1)
    pump_to(4, 0)

    for part in range(groups // half_g):
        fill(part, x_send)
        for g in range(part * half_g, (part + 1) * half_g):
            send_group(g, x_send, x_recv, x_ss, x_rs, 1)
    pump_to(4)
    x_recv[0] = x_send[0]

    sig0 = jax.nn.sigmoid(jnp.sum(hot0 * logits, axis=1, keepdims=True))
    sig1 = jax.nn.sigmoid(jnp.sum(hot1 * logits, axis=1, keepdims=True))
    gate0, gate1 = sig0 / (sig0 + sig1), sig1 / (sig0 + sig1)
    pump_to(5, 0)

    l_iota = lax.broadcasted_iota(jnp.int32, (T, GB), 1)
    for g in range(groups):
        for q in range(Q):
            at = l_iota + (g * GB - q * slots)
            val = jnp.where(at == icode0, gate0, 0.0) + jnp.where(at == icode1, gate1, 0.0)
            placeg[q * T : (q + 1) * T, g * GB : (g + 1) * GB] = val.astype(BF16)
    pump_to(5)

    o = lax.broadcasted_iota(jnp.int32, (GB, GB), 0)
    c = lax.broadcasted_iota(jnp.int32, (GB, GB), 1)
    want = ((o // slots) % GR) * RB + (o // GX) * slots + o % slots
    perm = (c == want).astype(F32).astype(BF16)

    def unpack(g, src, dst):
        got = dot(perm, src[pl.ds(g * GR, GR)].reshape(GB, DQ)).astype(BF16)
        for q in range(Q):
            dst[g * GX : (g + 1) * GX, q * DQ : (q + 1) * DQ] = got[q * GX : (q + 1) * GX, :]

    KB = rows_z * 2

    def matmul_rows(src, rows, c0, c1):
        def one(i, carry):
            cols = pl.ds(pl.multiple_of(i * KB, KB), KB)
            w = w_all[pl.ds(2 * i, 2), :, c0:c1].reshape(KB, c1 - c0)
            pre[rows, c0:c1] += dot(src[rows, cols], w)
            return carry

        lax.fori_loop(0, nz // 2, one, 0)

    pump_to(steps)
    pre[...] = jnp.zeros_like(pre)
    wait_bytes(g_recv.at[pl.ds(1, ns - 1)], g_sem.at[1])
    o16 = lax.broadcasted_iota(jnp.int32, (GX, GR * 16), 0)
    c16 = lax.broadcasted_iota(jnp.int32, (GX, GR * 16), 1)
    pick = (c16 == (o16 // slots) * 16 + o16 % slots).astype(F32).astype(BF16)
    for g in range(groups):
        got = dot(pick, g_recv[pl.ds(g * GR, GR)].reshape(GR * 16, 128))
        gcol[g * GX : (g + 1) * GX, :] = got[:, 0:1]
    for g in range(groups):
        wait_bytes(group_ref(g, c_recv), c_rs.at[g])
        unpack(g, c_recv, cs)
    R = ns * slots
    matmul_rows(cs, slice(0, R), 2 * FF, 3 * FF)
    first_half = groups // 2
    for g in range(first_half):
        wait_bytes(group_ref(g, x_recv), x_rs.at[g])
        unpack(g, x_recv, xs)
    cut = first_half * GX

    def row_gates(a, b):
        lane_r = lax.broadcasted_iota(jnp.int32, (b - a, n_exp), 1)
        row_logits = dot(xs[a:b, :], router_ref[...], 1, 1)
        own = jnp.sum(jnp.where(lane_r == ms, row_logits, 0.0), axis=1, keepdims=True)
        hit = lane_r.astype(F32) == gcol[a:b, :]
        other = jnp.sum(jnp.where(hit, row_logits, 0.0), axis=1, keepdims=True)
        own, other = jax.nn.sigmoid(own), jax.nn.sigmoid(other)
        gcol[a:b, :] = own / (own + other)

    if cut:
        matmul_rows(xs, slice(0, cut), 0, 2 * FF)
        row_gates(0, cut)
    for g in range(first_half, groups):
        wait_bytes(group_ref(g, x_recv), x_rs.at[g])
        unpack(g, x_recv, xs)
    matmul_rows(xs, slice(cut, R), 0, 2 * FF)
    row_gates(cut, R)
    gates = gcol[...]
    pre_gate = pre[:, 0:FF]
    pre_up = pre[:, FF : 2 * FF]
    d_hidden = pre[:, 2 * FF : 3 * FF] * gates
    sigma = jax.nn.sigmoid(pre_gate)
    act = pre_gate * sigma
    hidden = (act * pre_up).astype(BF16)
    hid[...] = hidden
    hidg[...] = (hidden.astype(F32) * gates).astype(BF16)
    dgu[:, 0:FF] = (d_hidden * pre_up * sigma * (1.0 + pre_gate * (1.0 - sigma))).astype(BF16)
    dgu[:, FF : 2 * FF] = (d_hidden * act).astype(BF16)

    half = rows_z // SUB

    def grad_of(chunk):
        cols = pl.ds(pl.multiple_of(chunk * rows_z, rows_z), rows_z)
        return dot(xs[:, cols], dgu[...], 0, 0), dot(cs[:, cols], hidg[...], 0, 0)

    def rs_copy(way, s, u):
        return pltpu.make_async_remote_copy(
            src_ref=rs_send.at[way, s, pl.ds(u * half, half)],
            dst_ref=rs_recv.at[way, s, pl.ds(u * half, half)],
            send_sem=rr_ss.at[way, s, u],
            recv_sem=rr_rs.at[way, s, u],
            device_id={"dp": near[way]},
            device_id_type=MESH,
        )

    def rs_used(way, s, u):
        return 0 <= s < steps and (s > 0 or far_half(way, u))

    def rs_order(way):
        return range(SUB - 1, -1, -1) if way == 0 else range(SUB)

    def rs_grads(s):
        at = [
            pl.ds(pl.multiple_of(chunk * rows_z, rows_z), rows_z)
            for chunk in ((mz + steps - s) % nz, (mz + nz - steps + s) % nz)
        ]
        if s == 0:
            at = at[:1]
        a = dot(jnp.concatenate([xs[:, c] for c in at], axis=1), dgu[...], 0, 0)
        b = dot(jnp.concatenate([cs[:, c] for c in at], axis=1), hidg[...], 0, 0)
        for way in range(len(at)):
            gbuf[way, :, 0 : 2 * FF] = a[way * rows_z : (way + 1) * rows_z]
            gbuf[way, :, 2 * FF : 3 * FF] = b[way * rows_z : (way + 1) * rows_z]

    def rs_piece(way, s, u):
        rows = slice(u * half, (u + 1) * half)
        val = gbuf[0 if s == 0 else way, rows, :]
        if rs_used(way, s - 1, u):
            rs_copy(way, s - 1, u).wait_recv()
            val = val + rs_recv[way, s - 1, rows, :].astype(F32)
        rs_send[way, s, rows, :] = val.astype(BF16)
        rs_copy(way, s, u).start()

    def rs_pieces(s, when):
        for i in range(SUB):
            for way in (0, 1):
                u = rs_order(way)[i]
                if rs_used(way, s, u) and when(rs_used(way, s - 1, u)):
                    rs_piece(way, s, u)

    def always(waits):
        return True

    rs_grads(0)
    rs_pieces(0, always)
    rs_grads(1)
    rs_pieces(1, lambda waits: not waits)

    for q in range(Q):
        n = nz // Q
        w_q = w_all[q * n : (q + 1) * n, :, 2 * FF : 3 * FF].reshape(DQ, FF)
        got = dot(hid[...], w_q, 1, 1).astype(BF16)
        for g in range(groups):
            eo[g, q * GX : (q + 1) * GX, :] = got[g * GX : (g + 1) * GX, :]
    for g in range(groups):
        r_send[pl.ds(g * GR, GR)] = dot(perm, eo[g], 0, 0).astype(BF16).reshape(GR, RB, DQ)
        send_group(g, r_send, r_recv, r_ss, r_rs, -1)
    r_recv[0] = r_send[0]

    rs_pieces(1, lambda waits: waits)
    first_mix = min(5, steps)

    for s in range(2, steps + 1):
        if s < steps:
            rs_grads(s)
            rs_pieces(s, always)
        if s == first_mix:
            for g in range(groups):
                wait_bytes(group_ref(g, r_recv), r_rs.at[g])
        for q in range(Q):
            if s == min(first_mix + q, steps):
                cols = slice(q * DQ, (q + 1) * DQ)
                back = r_recv[...].reshape(ns * RB, DQ)
                got = dot(placeg[q * T : (q + 1) * T, :], back)
                mixed_ref[0, :, cols] = (stream[:, cols] + got).astype(BF16)

    a, b = grad_of(mz)
    gbuf[0, :, 0 : 2 * FF] = a
    gbuf[0, :, 2 * FF : 3 * FF] = b
    flag = (train_ref[0] > 0).astype(F32)
    for way in (0, 1):
        for u in rs_order(way):
            rows = slice(u * half, (u + 1) * half)
            rs_copy(way, steps - 1, u).wait_recv()
            gbuf[0, rows, :] = gbuf[0, rows, :] + rs_recv[way, steps - 1, rows, :].astype(F32)
    gg_ref[0] = gbuf[0, :, 0:FF] * flag
    gu_ref[0] = gbuf[0, :, FF : 2 * FF] * flag
    gd_ref[0] = gbuf[0, :, 2 * FF : 3 * FF] * flag

    for way in (0, 1):
        for s in range(steps):
            for u in range(SUB):
                if ag_used(way, s, u):
                    ag_copy(way, s, u).wait_send()
                if rs_used(way, s, u):
                    rs_copy(way, s, u).wait_send()
    pair_a.wait_send()
    pair_b.wait_send()
    wait_bytes(cs_send.at[pl.ds(0, chips - 1)], p_sem.at[1, 0])
    wait_bytes(pf_send.at[pl.ds(0, chips - 1)], p_sem.at[2, 0])
    wait_bytes(c_send.at[pl.ds(1, ns - 1)], c_ss)
    wait_bytes(x_send.at[pl.ds(1, ns - 1)], x_ss)
    wait_bytes(g_send.at[pl.ds(1, ns - 1)], g_sem.at[0])
    wait_bytes(r_send.at[pl.ds(1, ns - 1)], r_ss)


def leave(*refs):
    n = len(refs) // 2
    sems = refs[-1]
    copies = [pltpu.make_async_copy(refs[i], refs[n + i], sems.at[i]) for i in range(n)]
    for c in copies:
        c.start()
    for c in copies:
        c.wait()


def body(
    grid3,
    nz,
    queries,
    keys,
    values,
    residual_in,
    cotangent,
    expert_ids,
    router,
    attn_gain,
    moe_gain,
    w_gate,
    w_up,
    w_down,
    trainable,
):
    ns = grid3[0] * grid3[1] * grid3[2]
    T, D = queries.shape[1:]
    H = D // HD
    FF = w_gate.shape[2]
    slots = max(2, 3 * T // ns)
    rows_z = w_gate.shape[1]
    RB, DQ, R = Q * slots, D // Q, ns * slots
    PR = H * HD // ns
    groups = ns // GR
    steps = nz // 2
    nc = grid3[2]
    chips = ns // nc
    vm = pltpu.VMEM
    dma = pltpu.SemaphoreType.DMA
    scratch = [
        dma((8,)),
        vm((T, D), BF16),
        vm((T, D), BF16),
        vm((T, D), BF16),
        vm((T, D), BF16),
        vm((T, D), BF16),
        vm((nz, rows_z, 3 * FF), BF16),
        vm((nc, chips, PR, HD), BF16),
        vm((chips, PR, HD), BF16),
        vm((chips, PR, HD), BF16),
        vm((chips, PR, HD), BF16),
        vm((chips, PR, HD), BF16),
        vm((chips, PR, HD), BF16),
        vm((chips, PR, HD), BF16),
        vm((nc, chips, PR, HD), BF16),
        vm((T, D), F32),
        vm((Q * T, DQ), BF16),
        vm((groups, GR * RB, Q * T), BF16),
        vm((Q * T, ns * RB), BF16),
        vm((ns, RB, DQ), BF16),
        vm((ns, RB, DQ), BF16),
        vm((ns, RB, DQ), BF16),
        vm((ns, RB, DQ), BF16),
        vm((ns, 16, 128), BF16),
        vm((ns, 16, 128), BF16),
        vm((R, D), BF16),
        vm((R, D), BF16),
        vm((R, 3 * FF), F32),
        vm((R, 1), F32),
        vm((R, 2 * FF), BF16),
        vm((R, FF), BF16),
        vm((R, FF), BF16),
        vm((ns, RB, DQ), BF16),
        vm((ns, RB, DQ), BF16),
        vm((groups, GR * RB, DQ), BF16),
        vm((2, rows_z, 3 * FF), F32),
        vm((2, steps, rows_z, 3 * FF), BF16),
        vm((2, steps, rows_z, 3 * FF), BF16),
        dma((2, steps, SUB)),
        dma((2, steps, SUB)),
        dma((4, 2)),
        dma(()),
        dma((groups,)),
        dma(()),
        dma((groups,)),
        dma((2,)),
        dma(()),
        dma((groups,)),
        dma((2, steps, SUB)),
        dma((2, steps, SUB)),
    ]
    anywhere = pl.BlockSpec(memory_space=pl.ANY)
    in_vmem = pl.BlockSpec(memory_space=pltpu.VMEM)
    outs = pl.pallas_call(
        functools.partial(kernel, grid3, slots),
        out_shape=(
            pltpu.VMEM((1, T, D), BF16),
            pltpu.VMEM((1, rows_z, FF), F32),
            pltpu.VMEM((1, rows_z, FF), F32),
            pltpu.VMEM((1, rows_z, FF), F32),
        ),
        in_specs=[anywhere] * 5
        + [in_vmem] * 4
        + [anywhere] * 3
        + [pl.BlockSpec(memory_space=pltpu.SMEM)],
        out_specs=(in_vmem,) * 4,
        scratch_shapes=scratch,
        compiler_params=pltpu.CompilerParams(
            collective_id=0, has_side_effects=True, vmem_limit_bytes=60 * 1024 * 1024
        ),
        name="layer",
    )(
        queries,
        keys,
        values,
        residual_in,
        cotangent,
        jnp.transpose(expert_ids, (0, 2, 1)),
        router.T,
        attn_gain.reshape(1, D),
        moe_gain.reshape(1, D),
        w_gate,
        w_up,
        w_down,
        trainable,
    )
    return pl.pallas_call(
        leave,
        out_shape=tuple(jax.ShapeDtypeStruct(o.shape, o.dtype) for o in outs),
        in_specs=[in_vmem] * len(outs),
        out_specs=(anywhere,) * len(outs),
        scratch_shapes=[dma((len(outs),))],
        name="leave",
    )(*(pltpu.with_memory_space_constraint(o, pltpu.VMEM) for o in outs))


def solution(mesh, grid3=(4, 4, 2)):
    blocks = P("dp", "seq", None)
    weights = P("seq", "dp", None)
    return jax.shard_map(
        functools.partial(body, grid3, mesh.shape["dp"]),
        mesh=mesh,
        in_specs=(blocks,) * 6 + (P(), P(), P()) + (weights,) * 3 + (P("seq"),),
        out_specs=(blocks, weights, weights, weights),
        check_vma=False,
    )
```
